128 devices in a mesh: row: 8 (over x, y_lo), col: 16 (over z, y_hi, core).
Axes of the slice: x: 4, y: 4 (y_hi: 2, y_lo: 2; y = y_hi * 2 + y_lo), z: 4, core: 2. Of those that a mesh axis runs over, the one named last changes fastest.
Arguments:
- pair: bfloat16 [512, 512, 128], P('row', 'col'), may hold values from -6 to 6
- ln_in: float32 [2, 128], replicated, may hold values from 0.5 to 1.5
- w_left: bfloat16 [2, 128, 256], replicated, may hold values from -0.5 to 0.5
- w_right: bfloat16 [2, 128, 256], replicated, may hold values from -0.5 to 0.5
- w_gate: bfloat16 [2, 128, 128], replicated, may hold values from -0.5 to 0.5
- ln_out: float32 [2, 128], replicated, may hold values from 0.5 to 1.5
- w_out: bfloat16 [2, 128, 128], replicated, may hold values from -0.5 to 0.5
Outputs:
- updated: bfloat16 [512, 512, 128], P('row', 'col')
The draws below stay inside these ranges and needn't reach their ends.
All inputs are finite; a program needn't handle non-finite values.
Results may differ from the reference program's by a relative error of at most 0.022.
Values may be sent and summed in bfloat16 or wider, within the bound.
A program may use at most 128 MiB of HBM per device.

```python
import jax
import jax.numpy as jnp
from jax import lax

C = 128
H = 128
N = 512


def block_scale(key, dims, pieces, low, largest):
    factor_of, own = 1.0, jax.random.fold_in(key, 6)
    for axis_at, parts in pieces:
        heights = jnp.exp(jax.random.uniform(jax.random.fold_in(own, axis_at), (parts,), jnp.float32, low / len(pieces), largest / len(pieces)))
        factor_of = factor_of * jnp.repeat(heights, dims[axis_at] // parts).reshape([-1 if axis == axis_at else 1 for axis in range(len(dims))])
    return factor_of


def scatter_about(rng, extent, width, most, shards=(), dtype=jnp.bfloat16):
    array = width * jax.random.normal(rng, extent, jnp.float32)
    if shards:
        array = array * block_scale(rng, extent, shards, -0.22, 0.18)
    return jnp.clip(array, -most, most).astype(dtype)


def setup_inputs(seed: int = 0) -> dict:
    seeds = jax.random.split(jax.random.key(seed), 8)
    return {
        "pair": scatter_about(seeds[0], (N, N, C), 1.0, 6.0, ((0, 8), (1, 16))),
        "ln_in": jnp.clip(jax.random.uniform(seeds[1], (2, C), jnp.float32, 0.5, 1.5), 0.5, 1.5),
        "w_left": scatter_about(seeds[2], (2, C, 2 * H), C ** -0.5, 0.5),
        "w_right": scatter_about(seeds[3], (2, C, 2 * H), C ** -0.5, 0.5),
        "w_gate": scatter_about(seeds[4], (2, C, C), C ** -0.5, 0.5),
        "ln_out": jnp.clip(jax.random.uniform(seeds[5], (2, H), jnp.float32, 0.5, 1.5), 0.5, 1.5),
        "w_out": scatter_about(seeds[6], (2, H, C), H ** -0.5, 0.5),
    }


def layer_norm(values, gain):
    mean = lax.optimization_barrier(jnp.mean(values, axis=-1, keepdims=True))
    centred = values - mean
    spread = lax.optimization_barrier(jnp.mean(centred * centred, axis=-1, keepdims=True))
    return centred * jax.lax.rsqrt(spread + 1e-05) * gain

def project(tile, gain, w_left, w_right, w_gate):
    normed = layer_norm(tile.astype(jnp.float32), gain).astype(jnp.bfloat16)
    hidden = w_left.shape[1] // 2
    pl = jnp.dot(normed, w_left, preferred_element_type=jnp.float32)
    pr = jnp.dot(normed, w_right, preferred_element_type=jnp.float32)
    left = (jax.nn.sigmoid(pl[..., :hidden]) * pl[..., hidden:]).astype(jnp.bfloat16)
    right = (jax.nn.sigmoid(pr[..., :hidden]) * pr[..., hidden:]).astype(jnp.bfloat16)
    gate = jax.nn.sigmoid(jnp.dot(normed, w_gate, preferred_element_type=jnp.float32))
    return (left, right, gate)

def finish(tile, edges, gate, gain, w_out):
    scaled = layer_norm(edges, gain).astype(jnp.bfloat16)
    update = jnp.dot(scaled, w_out, preferred_element_type=jnp.float32)
    return (tile.astype(jnp.float32) + gate * update).astype(jnp.bfloat16)

def reference(pair, ln_in, w_left, w_right, w_gate, ln_out, w_out):
    left, right, gate = project(pair, ln_in[0], w_left[0], w_right[0], w_gate[0])
    edges = jnp.einsum('ikh,jkh->ijh', left.astype(jnp.float32), right.astype(jnp.float32))
    middle = finish(pair, edges, gate, ln_out[0], w_out[0])
    left, right, gate = project(middle, ln_in[1], w_left[1], w_right[1], w_gate[1])
    edges = jnp.einsum('kih,kjh->ijh', left.astype(jnp.float32), right.astype(jnp.float32))
    return finish(middle, edges, gate, ln_out[1], w_out[1])
```

```python
import functools

import jax
import jax.numpy as jnp
from jax import lax
from jax.experimental import pallas as pl
from jax.experimental.pallas import tpu as pltpu
from jax.sharding import PartitionSpec as P


MESH = pl.DeviceIdType.MESH
F32, BF16 = jnp.float32, jnp.bfloat16
EPS = 1e-05


def place():
    row, col = lax.axis_index("row"), lax.axis_index("col")
    return row // 2, ((col // 2) % 2) * 2 + row % 2, col // 4, col % 2


def device_at(x, y, z, core):
    return x * 2 + y % 2, z * 4 + (y // 2) * 2 + core


def channel_at(x, y, z, core):
    return (((x + y + z) % 4) * 2 + core) * 16 + y * 4 + z


def norm_rows(values, gain):
    mean = jnp.mean(values, axis=0, keepdims=True)
    centred = values - mean
    spread = jnp.mean(centred * centred, axis=0, keepdims=True)
    return centred * lax.rsqrt(spread + EPS) * gain


def turned(matrix):
    return jnp.transpose(matrix.astype(F32))


def swap_halves(first, second):
    low = jnp.concatenate([first[:, :64], second[:, :64]], axis=1)
    high = jnp.concatenate([first[:, 64:], second[:, 64:]], axis=1)
    return low, high


def kernel(
    pair_ref, ln_in_ref, w_left_ref, w_right_ref, w_gate_ref, ln_out_ref, w_out_ref, out_ref,
    flat, tile, normed, gate, spread_buf, w_proj, w_turn, mat_l, mat_r,
    send_l, send_r, send_e, recv_l, recv_r, recv_e, send_sem, recv_sem,
):
    x, y, z, core = place()
    me_row, me_col = lax.axis_index("row"), lax.axis_index("col")
    me = me_row * 16 + me_col
    my_channel = channel_at(x, y, z, core)

    def partner(step, e):
        da, db = 3 - step // 2, 1 - step % 2
        dy, dz = 3 - e // 4, 3 - e % 4
        py, pz = (y + dy) % 4, (z + dz) % 4
        px = (x + da - dy - dz + 8) % 4
        return px, py, pz, (core + db) % 2

    barrier = pltpu.get_barrier_semaphore()

    def greet(n, carry):
        pr, pc = device_at(*partner(n // 16, n % 16))
        pl.semaphore_signal(barrier, inc=1, device_id=(pr, pc), device_id_type=MESH)
        return carry

    lax.fori_loop(0, 127, greet, 0)

    flat[...] = pair_ref[...].reshape(2048, 128).astype(F32)
    for u in range(2):
        left, right = turned(w_left_ref[u]).astype(BF16), turned(w_right_ref[u]).astype(BF16)
        for j in range(8):
            w_proj[u, 0, j, 0:16] = left[16 * j : 16 * j + 16]
            w_proj[u, 0, j, 16:32] = left[128 + 16 * j : 144 + 16 * j]
            w_proj[u, 1, j, 0:16] = right[16 * j : 16 * j + 16]
            w_proj[u, 1, j, 16:32] = right[128 + 16 * j : 144 + 16 * j]
        w_turn[u, 0] = turned(w_gate_ref[u]).astype(BF16)
        w_turn[u, 1] = turned(w_out_ref[u]).astype(BF16)

    def gain_of(ref, u):
        return jnp.transpose(jnp.broadcast_to(ref[u : u + 1, :], (128, 128)))

    gain_in = gain_of(ln_in_ref, 0)
    for s in range(16):
        block = jnp.concatenate(
            [flat[pl.ds(s, 64, stride=32), :], flat[pl.ds(16 + s, 64, stride=32), :]], axis=0
        )
        block = jnp.transpose(block)
        tile[:, s * 128 : s * 128 + 128] = block.astype(BF16)
        normed[:, s * 128 : s * 128 + 128] = norm_rows(block, gain_in).astype(BF16)

    pl.semaphore_wait(barrier, 127)

    def start(src, dst, slot, u, n, step, e, peer):
        pr, pc = device_at(*peer)

        @pl.when((step < 7) | (e < 15))
        def _():
            pltpu.make_async_remote_copy(
                src_ref=src,
                dst_ref=dst,
                send_sem=send_sem.at[u, n],
                recv_sem=recv_sem.at[u, n],
                device_id=(pr, pc),
                device_id_type=MESH,
            ).start()

        @pl.when((step == 7) & (e == 15))
        def _():
            pltpu.make_async_copy(src, dst, recv_sem.at[u, n]).start()

    for u in range(2):

        def project(side, send, recv, n):
            def step_body(step, carry):
                da, db = 3 - step // 2, 1 - step % 2
                j = ((x + y + z + da) % 4) * 2 + (core + db) % 2
                p = jnp.dot(w_proj[u, side, j], normed[...], preferred_element_type=F32)
                value = jax.nn.sigmoid(p[:16]) * p[16:]
                for s in range(16):
                    spread_buf[pl.ds(s, 16, stride=16), :] = value[:, s * 128 : s * 128 + 128]
                send[u, pl.ds(pl.multiple_of(j * 256, 256), 256), :] = spread_buf[0:256, :].astype(BF16)
                for e in range(16):
                    peer = partner(step, e)
                    there = pl.multiple_of(channel_at(*peer) * 16, 16)
                    here = pl.multiple_of(me * 16, 16)
                    start(
                        send.at[u, pl.ds(there, 16), :], recv.at[u, pl.ds(here, 16), :],
                        None, u, n, step, e, peer,
                    )
                return carry

            lax.fori_loop(0, 8, step_body, 0)

        project(1, send_r, recv_r, 0)
        project(0, send_l, recv_l, 1)

        gate[...] = jax.nn.sigmoid(jnp.dot(w_turn[u, 0], normed[...], preferred_element_type=F32))

        def gather(recv, mat):
            def body(c, carry):
                for m in range(4):
                    first = recv[u, pl.ds(pl.multiple_of((32 * m + c) * 16, 16), 16), :]
                    second = recv[u, pl.ds(pl.multiple_of((32 * m + 16 + c) * 16, 16), 16), :]
                    low, high = swap_halves(first, second)
                    mat[pl.ds(pl.multiple_of(c * 32, 32), 16), m * 128 : m * 128 + 128] = low
                    mat[pl.ds(pl.multiple_of(c * 32 + 16, 16), 16), m * 128 : m * 128 + 128] = high
                return carry

            lax.fori_loop(0, 16, body, 0)

        def arrived(recv, n):
            pltpu.make_async_copy(recv.at[u], recv.at[u], recv_sem.at[u, n]).wait()

        arrived(recv_r, 0)
        gather(recv_r, mat_r)
        if u == 0:
            mat_r[...] = jnp.transpose(mat_r[...].astype(F32)).astype(BF16)
        arrived(recv_l, 1)
        gather(recv_l, mat_l)
        contract = (((1,), (0,)), ((), ())) if u == 0 else (((1,), (1,)), ((), ()))
        for c4 in range(4):
            edges = lax.dot_general(
                mat_r[c4 * 128 : c4 * 128 + 128, :], mat_l[...], contract, preferred_element_type=F32
            ).astype(BF16)
            for c in range(4):
                for m in range(4):
                    low, high = swap_halves(
                        edges[c * 32 : c * 32 + 16, m * 128 : m * 128 + 128],
                        edges[c * 32 + 16 : c * 32 + 32, m * 128 : m * 128 + 128],
                    )
                    at = (32 * m + 4 * c4 + c) * 16
                    send_e[u, at : at + 16, :] = low
                    send_e[u, at + 256 : at + 272, :] = high

        def back(step, carry):
            for e in range(16):
                peer = partner(step, e)
                pr, pc = device_at(*peer)
                there = pl.multiple_of((pr * 16 + pc) * 16, 16)
                here = pl.multiple_of(my_channel * 16, 16)
                start(
                    send_e.at[u, pl.ds(there, 16), :], recv_e.at[u, pl.ds(here, 16), :],
                    None, u, 2, step, e, peer,
                )
            return carry

        lax.fori_loop(0, 8, back, 0)
        gain_out = gain_of(ln_out_ref, u)
        gain_next = gain_of(ln_in_ref, 1)
        arrived(recv_e, 2)
        spread_buf[...] = recv_e[u].astype(F32)
        for s in range(16):
            lanes = slice(s * 128, s * 128 + 128)
            scaled = norm_rows(spread_buf[pl.ds(s, 128, stride=16), :], gain_out).astype(BF16)
            update = jnp.dot(w_turn[u, 1], scaled, preferred_element_type=F32)
            updated = tile[:, lanes].astype(F32) + gate[:, lanes] * update
            if u == 0:
                rounded = updated.astype(BF16)
                tile[:, lanes] = rounded
                normed[:, lanes] = norm_rows(rounded.astype(F32), gain_next).astype(BF16)
            else:
                block = jnp.transpose(updated)
                flat[pl.ds(s, 64, stride=32), :] = block[:64]
                flat[pl.ds(16 + s, 64, stride=32), :] = block[64:]
    out_ref[...] = flat[...].astype(BF16).reshape(64, 32, 128)

    for u in range(2):
        for n, send in enumerate((send_r, send_l, send_e)):
            sent = send.at[u, pl.ds(0, 127 * 16), :]
            pltpu.make_async_copy(sent, sent, send_sem.at[u, n]).wait()


def local(pair, ln_in, w_left, w_right, w_gate, ln_out, w_out):
    tokens = pltpu.VMEM((2, 2048, 128), BF16)
    return pl.pallas_call(
        kernel,
        out_shape=jax.ShapeDtypeStruct((64, 32, 128), BF16),
        in_specs=[pl.BlockSpec(memory_space=pltpu.VMEM)] * 7,
        out_specs=pl.BlockSpec(memory_space=pltpu.VMEM),
        scratch_shapes=[
            pltpu.VMEM((2048, 128), F32),
            pltpu.VMEM((128, 2048), BF16),
            pltpu.VMEM((128, 2048), BF16),
            pltpu.VMEM((128, 2048), F32),
            pltpu.VMEM((2048, 128), F32),
            pltpu.VMEM((2, 2, 8, 32, 128), BF16),
            pltpu.VMEM((2, 2, 128, 128), BF16),
            pltpu.VMEM((512, 512), BF16),
            pltpu.VMEM((512, 512), BF16),
            tokens, tokens, tokens, tokens, tokens, tokens,
            pltpu.SemaphoreType.DMA((2, 3)),
            pltpu.SemaphoreType.DMA((2, 3)),
        ],
        compiler_params=pltpu.CompilerParams(
            collective_id=0, has_side_effects=True, vmem_limit_bytes=48 << 20
        ),
        name="triangle",
    )(pair, ln_in, w_left, w_right, w_gate, ln_out, w_out)


def solution(mesh):
    return jax.shard_map(
        local,
        mesh=mesh,
        in_specs=(P("row", "col", None), P(), P(), P(), P(), P(), P()),
        out_specs=P("row", "col", None),
        check_vma=False,
    )
```

```python
import functools

import jax
import jax.numpy as jnp
from jax import lax
from jax.experimental import pallas as pl
from jax.experimental.pallas import tpu as pltpu
from jax.sharding import PartitionSpec as P


MESH = pl.DeviceIdType.MESH
F32, BF16 = jnp.float32, jnp.bfloat16
EPS = 1e-05
FAR = (2, 1, 3, 0)


def norm_rows(values, gain):
    mean = jnp.mean(values, axis=0, keepdims=True)
    centred = values - mean
    spread = jnp.mean(centred * centred, axis=0, keepdims=True)
    return centred * lax.rsqrt(spread + EPS) * gain


def turned(matrix):
    return jnp.transpose(matrix.astype(F32))


def swap_halves(first, second):
    low = jnp.concatenate([first[:, :64], second[:, :64]], axis=1)
    high = jnp.concatenate([first[:, 64:], second[:, 64:]], axis=1)
    return low, high


def at(index, unit, count=1):
    return pl.ds(pl.multiple_of(index * unit, unit), unit * count)


def kernel(
    pair_hbm, ln_in_hbm, w_left_hbm, w_right_hbm, w_gate_hbm, ln_out_hbm, w_out_hbm, out_ref,
    pair_ref, ln_in_ref, w_left_ref, w_right_ref, w_gate_ref, ln_out_ref, w_out_ref,
    flat, tile, normed, gate, spread_buf, w_proj, w_turn, mat_l, mat_r,
    send_l, send_r, send_e, recv_l, recv_r, recv_e, load_sem, send_sem, recv_sem, edge_sem,
):
    row, col = lax.axis_index("row"), lax.axis_index("col")
    x, y, z, core = row // 2, ((col // 2) % 2) * 2 + row % 2, col // 4, col % 2
    xs = [(x + d) % 4 for d in range(4)]
    ys = [(y + d) % 4 for d in range(4)]
    zs = [(z + d) % 4 for d in range(4)]
    cores = [core, 1 - core]
    my_a = (x + y + z) % 4
    my_channel = (my_a * 2 + core) * 16 + y * 4 + z

    def device_at(px, py, pz, pcore):
        return px * 2 + py % 2, pz * 4 + (py // 2) * 2 + pcore

    loads = []
    pairs = (
        (pair_hbm, pair_ref), (ln_in_hbm, ln_in_ref), (w_right_hbm, w_right_ref), (w_left_hbm, w_left_ref),
        (w_gate_hbm, w_gate_ref), (ln_out_hbm, ln_out_ref), (w_out_hbm, w_out_ref),
    )
    for n, (src, dst) in enumerate(pairs):
        loads.append(pltpu.make_async_copy(src, dst, load_sem.at[n]))
        loads[-1].start()

    barrier = pltpu.get_barrier_semaphore()
    for dx in FAR:
        for dy in FAR:
            for dz in FAR:
                for dc in (1, 0):
                    if dx or dy or dz or dc:
                        pl.semaphore_signal(
                            barrier, inc=1, device_id=device_at(xs[dx], ys[dy], zs[dz], cores[dc]),
                            device_id_type=MESH,
                        )

    def prepare(u, side):
        both = turned((w_left_ref, w_right_ref)[side][u]).astype(BF16)
        for j in range(8):
            w_proj[u, side, j, 0:16] = both[16 * j : 16 * j + 16]
            w_proj[u, side, j, 16:32] = both[128 + 16 * j : 144 + 16 * j]

    def gain_of(ref, u):
        return jnp.transpose(jnp.broadcast_to(ref[u : u + 1, :], (128, 128)))

    loads[0].wait()
    loads[1].wait()
    flat[...] = pair_ref[...].reshape(2048, 128).astype(F32)
    gain_in = gain_of(ln_in_ref, 0)
    for s in range(16):
        block = jnp.concatenate(
            [flat[pl.ds(s, 64, stride=32), :], flat[pl.ds(16 + s, 64, stride=32), :]], axis=0
        )
        block = jnp.transpose(block)
        tile[:, s * 128 : s * 128 + 128] = block.astype(BF16)
        normed[:, s * 128 : s * 128 + 128] = norm_rows(block, gain_in).astype(BF16)
    loads[2].wait()
    prepare(0, 1)
    pl.semaphore_wait(barrier, 127)

    def send_to(src, dst, out_sem, in_sem, peer, may_be_me=None):
        def remote():
            pltpu.make_async_remote_copy(
                src_ref=src, dst_ref=dst, send_sem=out_sem, recv_sem=in_sem,
                device_id=device_at(*peer), device_id_type=MESH,
            ).start()

        if may_be_me is None:
            remote()
        else:
            pl.when(jnp.logical_not(may_be_me))(remote)
            pl.when(may_be_me)(lambda: pltpu.make_async_copy(src, dst, in_sem).start())

    for u in range(2):
        plane = (x, z)[u]
        slot = (row * 16 + col, col * 8 + row)[u]

        def project(side, order, send, recv):
            def step_body(step, carry):
                t, db = step // 2, 1 - step % 2
                a = (plane + t) % 4
                pcore = (core + db) % 2
                j = a * 2 + pcore
                p = jnp.dot(w_proj[u, side, j], normed[...], preferred_element_type=F32)
                value = jax.nn.sigmoid(p[:16]) * p[16:]
                for s in range(16):
                    spread_buf[pl.ds(s, 16, stride=16), :] = value[:, s * 128 : s * 128 + 128]
                send[u, at(j, 256), :] = spread_buf[0:256, :].astype(BF16)
                for dy in FAR:
                    for dz in FAR:
                        peer = ((a - ys[dy] - zs[dz] + 8) % 4, ys[dy], zs[dz], pcore)
                        there = j * 16 + ys[dy] * 4 + zs[dz]
                        send_to(
                            send.at[u, at(there, 16), :], recv.at[u, at(slot, 16), :],
                            send_sem.at[u, order], recv_sem.at[u, order, t], peer,
                            None if dy or dz else (a == my_a) & (db == 0),
                        )
                return carry

            lax.fori_loop(0, 8, step_body, 0)

        def arrived(recv, sem, count):
            some = recv.at[u, pl.ds(0, 16 * count), :]
            pltpu.make_async_copy(some, some, sem).wait()

        def gather(recv, mat, g):
            if u == 0:
                for c in range(16):
                    low, high = swap_halves(
                        recv[u, at(32 * g + c, 16), :], recv[u, at(32 * g + 16 + c, 16), :]
                    )
                    mat[c * 32 : c * 32 + 16, at(g, 128)] = low
                    mat[c * 32 + 16 : c * 32 + 32, at(g, 128)] = high
            else:
                for c in range(4):
                    for m in range(4):
                        slots = recv[u, at(32 * g + 8 * c + 2 * m, 16, 2), :]
                        low, high = swap_halves(slots[:16], slots[16:])
                        mat[at(8 * g + 2 * c, 16), m * 128 : m * 128 + 128] = low
                        mat[at(8 * g + 2 * c + 1, 16), m * 128 : m * 128 + 128] = high

        if u == 0:
            sides = ((1, send_r, recv_r, mat_r), (0, send_l, recv_l, mat_l))
        else:
            sides = ((0, send_l, recv_l, mat_l), (1, send_r, recv_r, mat_r))
        project(sides[0][0], 0, sides[0][1], sides[0][2])
        if u == 0:
            loads[3].wait()
            prepare(0, 0)
        project(sides[1][0], 1, sides[1][1], sides[1][2])

        if u == 0:
            prepare(1, 0)
            prepare(1, 1)
            for n in (4, 5, 6):
                loads[n].wait()
            for v in range(2):
                w_turn[v, 0] = turned(w_gate_ref[v]).astype(BF16)
                w_turn[v, 1] = turned(w_out_ref[v]).astype(BF16)
        gate[...] = jax.nn.sigmoid(jnp.dot(w_turn[u, 0], normed[...], preferred_element_type=F32))

        _, _, recv, mat = sides[0]

        def first_body(t, carry):
            arrived(recv, recv_sem.at[u, 0, t], 32)
            gather(recv, mat, (my_a - t + 4) % 4)
            return carry

        lax.fori_loop(0, 4, first_body, 0)
        if u == 0:
            mat_r[...] = jnp.transpose(mat_r[...].astype(F32)).astype(BF16)

        _, _, recv, mat = sides[1]

        def second_body(t, carry):
            g = (my_a - t + 4) % 4
            arrived(recv, recv_sem.at[u, 1, t], 32)
            gather(recv, mat, g)
            if u == 0:
                edges = jnp.dot(mat_r[...], mat_l[:, at(g, 128)], preferred_element_type=F32).astype(BF16)
                for c in range(16):
                    low, high = swap_halves(
                        edges[c * 32 : c * 32 + 16], edges[c * 32 + 16 : c * 32 + 32]
                    )
                    send_e[u, at(32 * g + c, 16), :] = low
                    send_e[u, at(32 * g + 16 + c, 16), :] = high
            else:
                edges = lax.dot_general(
                    mat_r[at(g, 128), :], mat_l[...], (((1,), (1,)), ((), ())), preferred_element_type=F32
                ).astype(BF16)
                for c in range(4):
                    for m in range(4):
                        lanes = slice(m * 128, m * 128 + 128)
                        low, high = swap_halves(
                            edges[c * 32 : c * 32 + 16, lanes], edges[c * 32 + 16 : c * 32 + 32, lanes]
                        )
                        send_e[u, at(32 * g + 8 * c + 2 * m, 16), :] = low
                        send_e[u, at(32 * g + 8 * c + 2 * m + 1, 16), :] = high
            for d in FAR:
                for dy in FAR:
                    for dc in (1, 0):
                        peer = (g, ys[dy], zs[d], cores[dc]) if u == 0 else (xs[d], ys[dy], g, cores[dc])
                        pr, pc = device_at(*peer)
                        there = (pr * 16 + pc, pc * 8 + pr)[u]
                        send_to(
                            send_e.at[u, at(there, 16), :], recv_e.at[u, at(my_channel, 16), :],
                            send_sem.at[u, 2], edge_sem.at[u], peer,
                            None if d or dy or dc else g == plane,
                        )
            return carry

        lax.fori_loop(0, 4, second_body, 0)

        gain_out = gain_of(ln_out_ref, u)
        gain_next = gain_of(ln_in_ref, 1)
        arrived(recv_e, edge_sem.at[u], 128)
        spread_buf[...] = recv_e[u].astype(F32)
        for s in range(16):
            lanes = slice(s * 128, s * 128 + 128)
            scaled = norm_rows(spread_buf[pl.ds(s, 128, stride=16), :], gain_out).astype(BF16)
            update = jnp.dot(w_turn[u, 1], scaled, preferred_element_type=F32)
            updated = tile[:, lanes].astype(F32) + gate[:, lanes] * update
            if u == 0:
                rounded = updated.astype(BF16)
                tile[:, lanes] = rounded
                normed[:, lanes] = norm_rows(rounded.astype(F32), gain_next).astype(BF16)
            else:
                block = jnp.transpose(updated)
                flat[pl.ds(s, 64, stride=32), :] = block[:64]
                flat[pl.ds(16 + s, 64, stride=32), :] = block[64:]
    out_ref[...] = flat[...].astype(BF16).reshape(64, 32, 128)

    for u in range(2):
        for n, send in enumerate((send_r, send_l, send_e)):
            sent = send.at[u, pl.ds(0, 127 * 16), :]
            pltpu.make_async_copy(sent, sent, send_sem.at[u, n]).wait()


def local(*args):
    tokens = pltpu.VMEM((2, 2048, 128), BF16)
    return pl.pallas_call(
        kernel,
        out_shape=jax.ShapeDtypeStruct((64, 32, 128), BF16),
        in_specs=[pl.BlockSpec(memory_space=pl.ANY)] * 7,
        out_specs=pl.BlockSpec(memory_space=pltpu.VMEM),
        scratch_shapes=[pltpu.VMEM(arg.shape, arg.dtype) for arg in args]
        + [
            pltpu.VMEM((2048, 128), F32),
            pltpu.VMEM((128, 2048), BF16),
            pltpu.VMEM((128, 2048), BF16),
            pltpu.VMEM((128, 2048), F32),
            pltpu.VMEM((2048, 128), F32),
            pltpu.VMEM((2, 2, 8, 32, 128), BF16),
            pltpu.VMEM((2, 2, 128, 128), BF16),
            pltpu.VMEM((512, 512), BF16),
            pltpu.VMEM((512, 512), BF16),
            tokens, tokens, tokens, tokens, tokens, tokens,
            pltpu.SemaphoreType.DMA((7,)),
            pltpu.SemaphoreType.DMA((2, 3)),
            pltpu.SemaphoreType.DMA((2, 2, 4)),
            pltpu.SemaphoreType.DMA((2,)),
        ],
        compiler_params=pltpu.CompilerParams(
            collective_id=0, has_side_effects=True, vmem_limit_bytes=48 << 20
        ),
        name="triangle",
    )(*args)


def solution(mesh):
    return jax.shard_map(
        local,
        mesh=mesh,
        in_specs=(P("row", "col", None), P(), P(), P(), P(), P(), P()),
        out_specs=P("row", "col", None),
        check_vma=False,
    )
```

```python
import itertools

import jax
import jax.numpy as jnp
from jax import lax
from jax.experimental import pallas as pl
from jax.experimental.pallas import tpu as pltpu
from jax.sharding import PartitionSpec as P


MESH = pl.DeviceIdType.MESH
F32, BF16 = jnp.float32, jnp.bfloat16
EPS = 1e-05
GROUPS = ((1, 3), (2, 0))


def hops(steps):
    return sum(min(d, 4 - d) for d in steps[:3])


ALL = sorted(itertools.product(range(4), range(4), range(4), range(2)), key=lambda d: (-hops(d), -d[3]))


def norm_rows(values, gain):
    mean = jnp.mean(values, axis=0, keepdims=True)
    centred = values - mean
    spread = jnp.mean(centred * centred, axis=0, keepdims=True)
    return centred * lax.rsqrt(spread + EPS) * gain


def turned(matrix):
    return jnp.transpose(matrix.astype(F32))


def swap_halves(first, second):
    low = jnp.concatenate([first[:, :64], second[:, :64]], axis=1)
    high = jnp.concatenate([first[:, 64:], second[:, 64:]], axis=1)
    return low, high


def at(index, unit, count=1):
    return pl.ds(pl.multiple_of(index * unit, unit), unit * count)


def kernel(
    pair_hbm, ln_in_hbm, w_left_hbm, w_right_hbm, w_gate_hbm, ln_out_hbm, w_out_hbm, out_ref,
    pair_ref, ln_in_ref, w_left_ref, w_right_ref, w_gate_ref, ln_out_ref, w_out_ref,
    flat, tile, normed, gate, spread_buf, w_proj, w_turn, right_t, left_low, left_high,
    send_l, send_r, send_e, recv_l, recv_r, recv_e,
    load_sem, send_sem, first_sem, second_sem, edge_sem,
):
    row, col = lax.axis_index("row"), lax.axis_index("col")
    x, y, z, core = row // 2, ((col // 2) % 2) * 2 + row % 2, col // 4, col % 2
    xs = [(x + d) % 4 for d in range(4)]
    ys = [(y + d) % 4 for d in range(4)]
    zs = [(z + d) % 4 for d in range(4)]
    cores = [core, 1 - core]
    y_low = [v % 2 for v in ys]
    y_high = [(v // 2) * 2 for v in ys]

    def device(steps):
        dx, dy, dz, dc = steps
        return xs[dx] * 2 + y_low[dy], zs[dz] * 4 + y_high[dy] + cores[dc]

    def channel(u, steps):
        dx, dy, dz, dc = steps
        plane, third = ((xs[dx], zs[dz]), (zs[dz], xs[dx]))[u]
        return (plane * 2 + cores[dc]) * 16 + ys[dy] * 4 + third

    loads = []
    pairs = (
        (pair_hbm, pair_ref), (ln_in_hbm, ln_in_ref), (w_right_hbm, w_right_ref), (w_left_hbm, w_left_ref),
        (w_gate_hbm, w_gate_ref), (ln_out_hbm, ln_out_ref), (w_out_hbm, w_out_ref),
    )
    for n, (src, dst) in enumerate(pairs):
        loads.append(pltpu.make_async_copy(src, dst, load_sem.at[n]))
        loads[-1].start()

    barrier = pltpu.get_barrier_semaphore()
    for steps in ALL:
        if any(steps):
            pl.semaphore_signal(barrier, inc=1, device_id=device(steps), device_id_type=MESH)

    def prepare(u, side):
        both = turned((w_left_ref, w_right_ref)[side][u]).astype(BF16)
        for j in range(4):
            w_proj[u, side, j, 0:32] = both[32 * j : 32 * j + 32]
            w_proj[u, side, j, 32:64] = both[128 + 32 * j : 160 + 32 * j]

    def gain_of(ref, u):
        return jnp.transpose(jnp.broadcast_to(ref[u : u + 1, :], (128, 128)))

    loads[0].wait()
    loads[1].wait()
    flat[...] = pair_ref[...].reshape(2048, 128).astype(F32)
    gain_in = gain_of(ln_in_ref, 0)
    for s in range(16):
        block = jnp.concatenate(
            [flat[pl.ds(s, 64, stride=32), :], flat[pl.ds(16 + s, 64, stride=32), :]], axis=0
        )
        block = jnp.transpose(block)
        tile[:, s * 128 : s * 128 + 128] = block.astype(BF16)
        normed[:, s * 128 : s * 128 + 128] = norm_rows(block, gain_in).astype(BF16)

    def send_to(src, dst, out_sem, in_sem, steps):
        if any(steps):
            pltpu.make_async_remote_copy(
                src_ref=src, dst_ref=dst, send_sem=out_sem, recv_sem=in_sem,
                device_id=device(steps), device_id_type=MESH,
            ).start()
        else:
            pltpu.make_async_copy(src, dst, in_sem).start()

    def project(u, side, plane, send):
        for part in range(4):
            p = jnp.dot(
                w_proj[u, side, plane], normed[:, part * 512 : part * 512 + 512], preferred_element_type=F32
            )
            value = jax.nn.sigmoid(p[:32]) * p[32:]
            for s in range(4):
                spread_buf[pl.ds(part * 4 + s, 32, stride=16), :] = value[:, s * 128 : s * 128 + 128]
        send[u, at(plane, 512), :] = spread_buf[0:512, :].astype(BF16)

    loads[2].wait()
    prepare(0, 1)

    def project_all(j, carry):
        project(0, 1, j, send_r)
        return carry

    lax.fori_loop(0, 4, project_all, 0)
    pl.semaphore_wait(barrier, 127)

    for u in range(2):
        axis = (0, 2)[u]
        planes = (xs, zs)[u]
        slot = (row * 16 + col, z * 32 + row * 4 + col % 4)[u]
        side, send, recv = ((1, send_r, recv_r), (0, send_l, recv_l))[u]

        def send_first(steps):
            send_to(
                send.at[u, at(channel(u, steps), 16), :], recv.at[u, at(slot, 16), :],
                send_sem.at[u, 0], first_sem.at[u, steps[axis]], steps,
            )

        if u == 0:
            for steps in ALL:
                send_first(steps)
        else:
            for d in GROUPS[0] + GROUPS[1]:
                project(u, side, planes[d], send)
                for steps in ALL:
                    if steps[axis] == d:
                        send_first(steps)

        side, send, recv = ((0, send_l, recv_l), (1, send_r, recv_r))[u]
        if u == 0:
            loads[3].wait()
            prepare(0, 0)
        for n, group in enumerate(GROUPS):
            for d in group:
                project(u, side, planes[d], send)
            for steps in ALL:
                if steps[axis] in group:
                    send_to(
                        send.at[u, at(channel(u, steps), 16), :], recv.at[u, at(slot, 16), :],
                        send_sem.at[u, 1], second_sem.at[u, n], steps,
                    )

        if u == 0:
            prepare(1, 0)
            prepare(1, 1)
            for n in (4, 5, 6):
                loads[n].wait()
            for v in range(2):
                w_turn[v, 0] = turned(w_gate_ref[v]).astype(BF16)
                w_turn[v, 1] = turned(w_out_ref[v]).astype(BF16)
        gate[...] = jax.nn.sigmoid(jnp.dot(w_turn[u, 0], normed[...], preferred_element_type=F32))

        def arrived(recv, sem, count):
            some = recv.at[u, pl.ds(0, 16 * count), :]
            pltpu.make_async_copy(some, some, sem).wait()

        for d in GROUPS[0] + GROUPS[1]:
            g = planes[-d % 4]
            if u == 0:
                arrived(recv_r, first_sem.at[u, d], 32)
                for half in range(2):
                    r = 2 * g + half
                    right_t[at(r, 128), :] = turned(recv_r[u, at(r, 256), :]).astype(BF16)
            else:
                arrived(recv_l, first_sem.at[u, d], 32)
                for r in range(8):
                    here = recv_l[u, at(32 * g + 4 * r, 16, 4), :]
                    none = jnp.zeros((64, 64), BF16)
                    lanes = slice(r * 128, r * 128 + 128)
                    for half in range(2):
                        part = here[:, half * 64 : half * 64 + 64]
                        low = jnp.concatenate([part, none], axis=1)
                        high = jnp.concatenate([none, part], axis=1)
                        for c in range(4):
                            rows = at(8 * g + 2 * c + half, 16)
                            left_low[rows, lanes] = low[c * 16 : c * 16 + 16]
                            left_high[rows, lanes] = high[c * 16 : c * 16 + 16]

        for n, group in enumerate(GROUPS):
            sources = [planes[-d % 4] for d in group]
            if u == 0:
                arrived(recv_l, second_sem.at[u, n], 64)
                left = jnp.concatenate(
                    [recv_l[u, at(2 * g + half, 256), :] for g in sources for half in range(2)], axis=1
                )
                is_low = lax.broadcasted_iota(jnp.int32, (16, 128), 1) < 64
                for r in range(8):
                    both = jnp.dot(
                        right_t[r * 128 : r * 128 + 128, :], left, preferred_element_type=F32
                    )
                    for k in range(4):
                        block = both[:, k * 128 : k * 128 + 128]
                        for c in range(2):
                            top = block[c * 32 : c * 32 + 32]
                            bottom = block[64 + c * 32 : 96 + c * 32]
                            edges = jnp.where(is_low, top[:16], bottom[16:]) + pltpu.roll(
                                jnp.where(is_low, top[16:], bottom[:16]), 64, 1
                            )
                            to = (n * 64 + k * 16 + 2 * r + c) * 16
                            send_e[u, to : to + 16, :] = edges.astype(BF16)
            else:
                arrived(recv_r, second_sem.at[u, n], 64)
                right = jnp.concatenate(
                    [
                        jnp.concatenate([recv_r[u, at(32 * g + 4 * r, 16, 4), :] for r in range(8)], axis=1)
                        for g in sources
                    ],
                    axis=0,
                )
                contract = (((1,), (1,)), ((), ()))
                first = lax.dot_general(right, left_low[...], contract, preferred_element_type=F32)
                second = lax.dot_general(right, left_high[...], contract, preferred_element_type=F32)
                first, second = first.astype(BF16), second.astype(BF16)
                for k in range(8):
                    for m in range(4):
                        part = (slice(k * 16, k * 16 + 16), slice(m * 128, m * 128 + 128))
                        low, high = swap_halves(first[part], second[part])
                        to = (n * 64 + k * 8 + 2 * m) * 16
                        send_e[u, to : to + 16, :] = low
                        send_e[u, to + 16 : to + 32, :] = high
            for steps in ALL:
                back = -steps[axis] % 4
                if back in group:
                    pr, pc = device(steps)
                    there = (pr % 2 * 16 + pc, pc % 4 * 8 + pr)[u] + (n * 2 + group.index(back)) * 32
                    send_to(
                        send_e.at[u, at(there, 16), :], recv_e.at[u, at(channel(u, (0, 0, 0, 0)), 16), :],
                        send_sem.at[u, 2], edge_sem.at[u], steps,
                    )

        gain_out = gain_of(ln_out_ref, u)
        gain_next = gain_of(ln_in_ref, 1)
        arrived(recv_e, edge_sem.at[u], 128)
        spread_buf[...] = recv_e[u].astype(F32)
        for s in range(16):
            lanes = slice(s * 128, s * 128 + 128)
            scaled = norm_rows(spread_buf[pl.ds(s, 128, stride=16), :], gain_out).astype(BF16)
            update = jnp.dot(w_turn[u, 1], scaled, preferred_element_type=F32)
            updated = tile[:, lanes].astype(F32) + gate[:, lanes] * update
            if u == 0:
                rounded = updated.astype(BF16)
                tile[:, lanes] = rounded
                normed[:, lanes] = norm_rows(rounded.astype(F32), gain_next).astype(BF16)
            else:
                block = jnp.transpose(updated)
                flat[pl.ds(s, 64, stride=32), :] = block[:64]
                flat[pl.ds(16 + s, 64, stride=32), :] = block[64:]
    out_ref[...] = flat[...].astype(BF16).reshape(64, 32, 128)

    for u in range(2):
        for n in range(3):
            sent = send_e.at[u, pl.ds(0, 127 * 16), :]
            pltpu.make_async_copy(sent, sent, send_sem.at[u, n]).wait()


def local(*args):
    tokens = pltpu.VMEM((2, 2048, 128), BF16)
    return pl.pallas_call(
        kernel,
        out_shape=jax.ShapeDtypeStruct((64, 32, 128), BF16),
        in_specs=[pl.BlockSpec(memory_space=pl.ANY)] * 7,
        out_specs=pl.BlockSpec(memory_space=pltpu.VMEM),
        scratch_shapes=[pltpu.VMEM(arg.shape, arg.dtype) for arg in args]
        + [
            pltpu.VMEM((2048, 128), F32),
            pltpu.VMEM((128, 2048), BF16),
            pltpu.VMEM((128, 2048), BF16),
            pltpu.VMEM((128, 2048), F32),
            pltpu.VMEM((2048, 128), F32),
            pltpu.VMEM((2, 2, 4, 64, 128), BF16),
            pltpu.VMEM((2, 2, 128, 128), BF16),
            pltpu.VMEM((1024, 256), BF16),
            pltpu.VMEM((512, 1024), BF16),
            pltpu.VMEM((512, 1024), BF16),
            tokens, tokens, tokens, tokens, tokens, tokens,
            pltpu.SemaphoreType.DMA((7,)),
            pltpu.SemaphoreType.DMA((2, 3)),
            pltpu.SemaphoreType.DMA((2, 4)),
            pltpu.SemaphoreType.DMA((2, 2)),
            pltpu.SemaphoreType.DMA((2,)),
        ],
        compiler_params=pltpu.CompilerParams(
            collective_id=0, has_side_effects=True, vmem_limit_bytes=48 << 20
        ),
        name="triangle",
    )(*[pltpu.with_memory_space_constraint(arg, pltpu.HBM) for arg in args])


def solution(mesh):
    return jax.shard_map(
        local,
        mesh=mesh,
        in_specs=(P("row", "col", None), P(), P(), P(), P(), P(), P()),
        out_specs=P("row", "col", None),
        check_vma=False,
    )
```

```python
import itertools

import jax
import jax.numpy as jnp
from jax import lax
from jax.experimental import pallas as pl
from jax.experimental.pallas import tpu as pltpu
from jax.sharding import PartitionSpec as P


MESH = pl.DeviceIdType.MESH
F32, BF16 = jnp.float32, jnp.bfloat16
EPS = 1e-05
GROUPS = ((1, 3), (2, 0))
OTHERS = ((1, 1), (1, 0), (0, 1), (0, 0))


def hops(steps):
    return sum(min(d, 4 - d) for d in steps[:3])


ALL = sorted(itertools.product(range(4), range(4), range(4), range(2)), key=lambda d: (-hops(d), -d[3]))


def norm_rows(values, gain):
    mean = jnp.mean(values, axis=0, keepdims=True)
    centred = values - mean
    spread = jnp.mean(centred * centred, axis=0, keepdims=True)
    return centred * lax.rsqrt(spread + EPS) * gain


def turned(matrix):
    return jnp.transpose(matrix.astype(F32))


def swap_halves(first, second):
    low = jnp.concatenate([first[:, :64], second[:, :64]], axis=1)
    high = jnp.concatenate([first[:, 64:], second[:, 64:]], axis=1)
    return low, high


def at(index, unit, count=1):
    return pl.ds(pl.multiple_of(index * unit, unit), unit * count)


def kernel(
    pair_hbm, ln_in_hbm, w_left_hbm, w_right_hbm, w_gate_hbm, ln_out_hbm, w_out_hbm, out_ref,
    pair_ref, ln_in_ref, w_left_ref, w_right_ref, w_gate_ref, ln_out_ref, w_out_ref,
    flat, tile, normed, gate, spread_buf, w_proj, w_turn, right_t, left_low, left_high,
    send_l, send_r, send_e, recv_l, recv_r, recv_e,
    load_sem, send_sem, first_sem, second_sem, edge_sem,
):
    row, col = lax.axis_index("row"), lax.axis_index("col")
    x, y, z, core = row // 2, ((col // 2) % 2) * 2 + row % 2, col // 4, col % 2
    xs = [(x + d) % 4 for d in range(4)]
    ys = [(y + d) % 4 for d in range(4)]
    zs = [(z + d) % 4 for d in range(4)]
    cores = [core, 1 - core]
    y_low = [v % 2 for v in ys]
    y_high = [(v // 2) * 2 for v in ys]

    def device(steps):
        dx, dy, dz, dc = steps
        return xs[dx] * 2 + y_low[dy], zs[dz] * 4 + y_high[dy] + cores[dc]

    def channel(u, steps):
        dx, dy, dz, dc = steps
        if u == 0:
            return (xs[dx] * 2 + cores[dc]) * 16 + ys[dy] * 4 + zs[dz]
        return (cores[dc] * 2 + xs[dx] % 2) * 32 + (xs[dx] // 2) * 16 + ys[dy] * 4 + zs[dz]

    def group_of(u, steps):
        return 1 - steps[0] % 2 if u == 0 else 1 - steps[3]

    loads = []
    pairs = (
        (pair_hbm, pair_ref), (ln_in_hbm, ln_in_ref), (w_right_hbm, w_right_ref), (w_left_hbm, w_left_ref),
        (w_gate_hbm, w_gate_ref), (ln_out_hbm, ln_out_ref), (w_out_hbm, w_out_ref),
    )
    for n, (src, dst) in enumerate(pairs):
        loads.append(pltpu.make_async_copy(src, dst, load_sem.at[n]))
        loads[-1].start()

    barrier = pltpu.get_barrier_semaphore()
    for steps in ALL:
        if any(steps):
            pl.semaphore_signal(barrier, inc=1, device_id=device(steps), device_id_type=MESH)

    def prepare(u, side):
        both = turned((w_left_ref, w_right_ref)[side][u]).astype(BF16)
        for j in range(4):
            w_proj[u, side, j, 0:32] = both[32 * j : 32 * j + 32]
            w_proj[u, side, j, 32:64] = both[128 + 32 * j : 160 + 32 * j]

    def gain_of(ref, u):
        return jnp.transpose(jnp.broadcast_to(ref[u : u + 1, :], (128, 128)))

    loads[0].wait()
    loads[1].wait()
    for ii in range(64):
        flat[ii * 40 : ii * 40 + 32, :] = pair_ref[ii].astype(F32)
    gain_in = gain_of(ln_in_ref, 0)
    for s in range(16):
        block = jnp.concatenate(
            [flat[pl.ds(s, 64, stride=40), :], flat[pl.ds(16 + s, 64, stride=40), :]], axis=0
        )
        block = jnp.transpose(block)
        tile[:, s * 128 : s * 128 + 128] = block.astype(BF16)
        normed[:, s * 128 : s * 128 + 128] = norm_rows(block, gain_in).astype(BF16)

    def send_to(src, dst, out_sem, in_sem, steps):
        if any(steps):
            pltpu.make_async_remote_copy(
                src_ref=src, dst_ref=dst, send_sem=out_sem, recv_sem=in_sem,
                device_id=device(steps), device_id_type=MESH,
            ).start()
        else:
            pltpu.make_async_copy(src, dst, in_sem).start()

    def project(u, side, chunk, send):
        for part in range(4):
            p = jnp.dot(
                w_proj[u, side, chunk], normed[:, part * 512 : part * 512 + 512], preferred_element_type=F32
            )
            value = jax.nn.sigmoid(p[:32]) * p[32:]
            for s in range(4):
                spread_buf[pl.ds(part * 4 + s, 32, stride=24), :] = value[:, s * 128 : s * 128 + 128]
        for h in range(32):
            send[u, at(chunk * 32 + h, 16), :] = spread_buf[h * 24 : h * 24 + 16, :].astype(BF16)

    loads[2].wait()
    prepare(0, 1)

    def project_all(j, carry):
        project(0, 1, j, send_r)
        return carry

    lax.fori_loop(0, 4, project_all, 0)
    pl.semaphore_wait(barrier, 127)

    for u in range(2):
        slot = (row * 16 + col, core * 64 + row * 8 + col // 2)[u]
        side, send, recv = ((1, send_r, recv_r), (0, send_l, recv_l))[u]

        def send_first(steps):
            send_to(
                send.at[u, at(channel(u, steps), 16), :], recv.at[u, at(slot, 16), :],
                send_sem.at[u, 0], first_sem.at[u, steps[3 * u]], steps,
            )

        if u == 0:
            for steps in ALL:
                send_first(steps)
        else:
            for dc, odd in OTHERS:
                project(u, side, cores[dc] * 2 + xs[odd] % 2, send)
                for steps in ALL:
                    if (steps[3], steps[0] % 2) == (dc, odd):
                        send_first(steps)

        side, send, recv = ((0, send_l, recv_l), (1, send_r, recv_r))[u]
        if u == 0:
            loads[3].wait()
            prepare(0, 0)
        for n, group in enumerate(GROUPS):
            for k in range(2):
                project(u, side, xs[group[k]] if u == 0 else cores[1 - n] * 2 + k, send)
            for steps in ALL:
                if group_of(u, steps) == n:
                    send_to(
                        send.at[u, at(channel(u, steps), 16), :], recv.at[u, at(slot, 16), :],
                        send_sem.at[u, 1], second_sem.at[u, n], steps,
                    )

        if u == 0:
            prepare(1, 0)
            prepare(1, 1)
            for n in (4, 5, 6):
                loads[n].wait()
            for v in range(2):
                w_turn[v, 0] = turned(w_gate_ref[v]).astype(BF16)
                w_turn[v, 1] = turned(w_out_ref[v]).astype(BF16)
        gate[...] = jax.nn.sigmoid(jnp.dot(w_turn[u, 0], normed[...], preferred_element_type=F32))

        def arrived(recv, sem, count):
            some = recv.at[u, pl.ds(0, 16 * count), :]
            pltpu.make_async_copy(some, some, sem).wait()

        for d in (1, 3, 2, 0) if u == 0 else (1, 0):
            if u == 0:
                g = xs[-d % 4]
                arrived(recv_r, first_sem.at[u, d], 32)
                for half in range(2):
                    r = 2 * g + half
                    right_t[at(r, 128), :] = turned(recv_r[u, at(r, 256), :]).astype(BF16)
            else:
                g = cores[d]
                arrived(recv_l, first_sem.at[u, d], 64)
                for r in range(8):
                    here = recv_l[u, at(64 * g + 8 * r, 16, 8), :]
                    none = jnp.zeros((128, 64), BF16)
                    lanes = slice(r * 128, r * 128 + 128)
                    for half in range(2):
                        part = here[:, half * 64 : half * 64 + 64]
                        low = jnp.concatenate([part, none], axis=1)
                        high = jnp.concatenate([none, part], axis=1)
                        for c in range(8):
                            rows = at(4 * c + 2 * g + half, 16)
                            left_low[rows, lanes] = low[c * 16 : c * 16 + 16]
                            left_high[rows, lanes] = high[c * 16 : c * 16 + 16]

        for n, group in enumerate(GROUPS):
            if u == 0:
                sources = [xs[-d % 4] for d in group]
                arrived(recv_l, second_sem.at[u, n], 64)
                left = jnp.concatenate(
                    [recv_l[u, at(2 * g + half, 256), :] for g in sources for half in range(2)], axis=1
                )
                is_low = lax.broadcasted_iota(jnp.int32, (16, 128), 1) < 64
                for r in range(8):
                    both = jnp.dot(
                        right_t[r * 128 : r * 128 + 128, :], left, preferred_element_type=F32
                    )
                    for k in range(4):
                        block = both[:, k * 128 : k * 128 + 128]
                        for c in range(2):
                            top = block[c * 32 : c * 32 + 32]
                            bottom = block[64 + c * 32 : 96 + c * 32]
                            edges = jnp.where(is_low, top[:16], bottom[16:]) + pltpu.roll(
                                jnp.where(is_low, top[16:], bottom[:16]), 64, 1
                            )
                            to = (n * 64 + k * 16 + 2 * r + c) * 16
                            send_e[u, to : to + 16, :] = edges.astype(BF16)
            else:
                arrived(recv_r, second_sem.at[u, n], 64)
                g = cores[1 - n]
                right = jnp.concatenate([recv_r[u, at(64 * g + 8 * r, 16, 8), :] for r in range(8)], axis=1)
                contract = (((1,), (1,)), ((), ()))
                first = lax.dot_general(right, left_low[...], contract, preferred_element_type=F32)
                second = lax.dot_general(right, left_high[...], contract, preferred_element_type=F32)
                first, second = first.astype(BF16), second.astype(BF16)
                for k in range(8):
                    for m in range(4):
                        part = (slice(k * 16, k * 16 + 16), slice(m * 128, m * 128 + 128))
                        low, high = swap_halves(first[part], second[part])
                        to = (n * 64 + k * 8 + 2 * m) * 16
                        send_e[u, to : to + 16, :] = low
                        send_e[u, to + 16 : to + 32, :] = high
            for steps in ALL:
                if group_of(u, steps) == n:
                    pr, pc = device(steps)
                    if u == 0:
                        there = (n * 2 + group.index(-steps[0] % 4)) * 32 + pr % 2 * 16 + pc
                    else:
                        there = n * 64 + (pc // 2) * 8 + pr
                    send_to(
                        send_e.at[u, at(there, 16), :], recv_e.at[u, at(channel(u, (0, 0, 0, 0)), 16), :],
                        send_sem.at[u, 2], edge_sem.at[u, n], steps,
                    )

        gain_out = gain_of(ln_out_ref, u)
        gain_next = gain_of(ln_in_ref, 1)
        for n, group in enumerate(GROUPS):
            arrived(recv_e, edge_sem.at[u, n], 64)
            for k in range(2):
                base = xs[group[k]] * 32 if u == 0 else cores[1 - n] * 64 + k * 32
                for h in range(32):
                    spread_buf[at(base * 3 + h * 3, 8, 2), :] = recv_e[u, at(base + h, 16), :].astype(F32)
        for s in range(16):
            lanes = slice(s * 128, s * 128 + 128)
            scaled = norm_rows(spread_buf[pl.ds(s, 128, stride=24), :], gain_out).astype(BF16)
            update = jnp.dot(w_turn[u, 1], scaled, preferred_element_type=F32)
            updated = tile[:, lanes].astype(F32) + gate[:, lanes] * update
            if u == 0:
                rounded = updated.astype(BF16)
                tile[:, lanes] = rounded
                normed[:, lanes] = norm_rows(rounded.astype(F32), gain_next).astype(BF16)
            else:
                block = jnp.transpose(updated)
                flat[pl.ds(s, 64, stride=40), :] = block[:64]
                flat[pl.ds(16 + s, 64, stride=40), :] = block[64:]
    for ii in range(64):
        out_ref[ii] = flat[ii * 40 : ii * 40 + 32, :].astype(BF16)

    for u in range(2):
        for n in range(3):
            sent = send_e.at[u, pl.ds(0, 127 * 16), :]
            pltpu.make_async_copy(sent, sent, send_sem.at[u, n]).wait()


def local(*args):
    tokens = pltpu.VMEM((2, 2048, 128), BF16)
    return pl.pallas_call(
        kernel,
        out_shape=jax.ShapeDtypeStruct((64, 32, 128), BF16),
        in_specs=[pl.BlockSpec(memory_space=pl.ANY)] * 7,
        out_specs=pl.BlockSpec(memory_space=pltpu.VMEM),
        scratch_shapes=[pltpu.VMEM(arg.shape, arg.dtype) for arg in args]
        + [
            pltpu.VMEM((64 * 40, 128), F32),
            pltpu.VMEM((128, 2048), BF16),
            pltpu.VMEM((128, 2048), BF16),
            pltpu.VMEM((128, 2048), F32),
            pltpu.VMEM((128 * 24, 128), F32),
            pltpu.VMEM((2, 2, 4, 64, 128), BF16),
            pltpu.VMEM((2, 2, 128, 128), BF16),
            pltpu.VMEM((1024, 256), BF16),
            pltpu.VMEM((512, 1024), BF16),
            pltpu.VMEM((512, 1024), BF16),
            tokens, tokens, tokens, tokens, tokens, tokens,
            pltpu.SemaphoreType.DMA((7,)),
            pltpu.SemaphoreType.DMA((2, 3)),
            pltpu.SemaphoreType.DMA((2, 4)),
            pltpu.SemaphoreType.DMA((2, 2)),
            pltpu.SemaphoreType.DMA((2, 2)),
        ],
        compiler_params=pltpu.CompilerParams(
            collective_id=0, has_side_effects=True, vmem_limit_bytes=48 << 20
        ),
        name="triangle",
    )(*[pltpu.with_memory_space_constraint(arg, pltpu.HBM) for arg in args])


def solution(mesh):
    return jax.shard_map(
        local,
        mesh=mesh,
        in_specs=(P("row", "col", None), P(), P(), P(), P(), P(), P()),
        out_specs=P("row", "col", None),
        check_vma=False,
    )
```

```python
import itertools

import jax
import jax.numpy as jnp
from jax import lax
from jax.experimental import pallas as pl
from jax.experimental.pallas import tpu as pltpu
from jax.sharding import PartitionSpec as P


MESH = pl.DeviceIdType.MESH
F32, BF16 = jnp.float32, jnp.bfloat16
EPS = 1e-05
GROUPS = ((1, 3), (2, 0))
OTHERS = ((1, 1), (1, 0), (0, 1), (0, 0))


def hops(steps):
    return sum(min(d, 4 - d) for d in steps[:3])


ALL = sorted(itertools.product(range(4), range(4), range(4), range(2)), key=lambda d: (-hops(d), -d[3]))


def norm_rows(values, gain):
    mean = jnp.mean(values, axis=0, keepdims=True)
    centred = values - mean
    spread = jnp.mean(centred * centred, axis=0, keepdims=True)
    return centred * lax.rsqrt(spread + EPS) * gain


def turned(matrix):
    return jnp.transpose(matrix.astype(F32))


def swap_halves(first, second):
    low = jnp.concatenate([first[:, :64], second[:, :64]], axis=1)
    high = jnp.concatenate([first[:, 64:], second[:, 64:]], axis=1)
    return low, high


def at(index, unit, count=1):
    return pl.ds(pl.multiple_of(index * unit, unit), unit * count)


def kernel(
    pair_hbm, ln_in_hbm, w_left_hbm, w_right_hbm, w_gate_hbm, ln_out_hbm, w_out_hbm, out_ref,
    pair_ref, ln_in_ref, w_left_ref, w_right_ref, w_gate_ref, ln_out_ref, w_out_ref,
    flat, tile, normed, gate, spread_buf, w_proj, w_turn, right_t, left_rows,
    send_l, send_r, send_e, recv_l, recv_r, recv_e,
    load_sem, send_sem, first_sem, second_sem, edge_sem,
):
    row, col = lax.axis_index("row"), lax.axis_index("col")
    x, y, z, core = row // 2, ((col // 2) % 2) * 2 + row % 2, col // 4, col % 2
    xs = [(x + d) % 4 for d in range(4)]
    ys = [(y + d) % 4 for d in range(4)]
    zs = [(z + d) % 4 for d in range(4)]
    cores = [core, 1 - core]
    y_low = [v % 2 for v in ys]
    y_high = [(v // 2) * 2 for v in ys]

    def device(steps):
        dx, dy, dz, dc = steps
        return xs[dx] * 2 + y_low[dy], zs[dz] * 4 + y_high[dy] + cores[dc]

    def channel(u, steps):
        dx, dy, dz, dc = steps
        if u == 0:
            return (xs[dx] * 2 + cores[dc]) * 16 + ys[dy] * 4 + zs[dz]
        return (cores[dc] * 2 + xs[dx] % 2) * 32 + (xs[dx] // 2) * 16 + ys[dy] * 4 + zs[dz]

    def group_of(u, steps):
        return 1 - steps[0] % 2 if u == 0 else 1 - steps[3]

    loads = []
    pairs = (
        (pair_hbm, pair_ref), (ln_in_hbm, ln_in_ref), (w_right_hbm, w_right_ref), (w_left_hbm, w_left_ref),
        (w_gate_hbm, w_gate_ref), (ln_out_hbm, ln_out_ref), (w_out_hbm, w_out_ref),
    )
    for n, (src, dst) in enumerate(pairs):
        loads.append(pltpu.make_async_copy(src, dst, load_sem.at[n]))
        loads[-1].start()

    barrier = pltpu.get_barrier_semaphore()
    for steps in ALL:
        if any(steps):
            pl.semaphore_signal(barrier, inc=1, device_id=device(steps), device_id_type=MESH)

    def prepare(u, side):
        both = turned((w_left_ref, w_right_ref)[side][u]).astype(BF16)
        for j in range(4):
            w_proj[u, side, j, 0:32] = both[32 * j : 32 * j + 32]
            w_proj[u, side, j, 32:64] = both[128 + 32 * j : 160 + 32 * j]

    def gain_of(ref, u):
        return jnp.transpose(jnp.broadcast_to(ref[u : u + 1, :], (128, 128)))

    loads[0].wait()
    loads[1].wait()
    for ii in range(64):
        flat[ii * 40 : ii * 40 + 32, :] = pair_ref[ii].astype(F32)
    gain_in = gain_of(ln_in_ref, 0)
    for s in range(16):
        block = jnp.concatenate(
            [flat[pl.ds(s, 64, stride=40), :], flat[pl.ds(16 + s, 64, stride=40), :]], axis=0
        )
        block = jnp.transpose(block)
        tile[:, s * 128 : s * 128 + 128] = block.astype(BF16)
        normed[:, s * 128 : s * 128 + 128] = norm_rows(block, gain_in).astype(BF16)

    def send_to(src, dst, out_sem, in_sem, steps):
        if any(steps):
            pltpu.make_async_remote_copy(
                src_ref=src, dst_ref=dst, send_sem=out_sem, recv_sem=in_sem,
                device_id=device(steps), device_id_type=MESH,
            ).start()
        else:
            pltpu.make_async_copy(src, dst, in_sem).start()

    def project(u, side, chunk, send):
        for part in range(4):
            p = jnp.dot(
                w_proj[u, side, chunk], normed[:, part * 512 : part * 512 + 512], preferred_element_type=F32
            )
            value = jax.nn.sigmoid(p[:32]) * p[32:]
            for s in range(4):
                spread_buf[pl.ds(part * 4 + s, 32, stride=24), :] = value[:, s * 128 : s * 128 + 128]
        for h in range(32):
            send[u, at(chunk * 32 + h, 16), :] = spread_buf[h * 24 : h * 24 + 16, :].astype(BF16)

    loads[2].wait()
    prepare(0, 1)

    def project_all(j, carry):
        project(0, 1, j, send_r)
        return carry

    lax.fori_loop(0, 4, project_all, 0)
    pl.semaphore_wait(barrier, 127)

    for u in range(2):
        slot = (row * 16 + col, core * 64 + row * 8 + col // 2)[u]
        side, send, recv = ((1, send_r, recv_r), (0, send_l, recv_l))[u]

        def send_first(steps):
            send_to(
                send.at[u, at(channel(u, steps), 16), :], recv.at[u, at(slot, 16), :],
                send_sem.at[u, 0], first_sem.at[u, steps[3 * u]], steps,
            )

        if u == 0:
            for steps in ALL:
                send_first(steps)
        else:
            for dc, odd in OTHERS:
                project(u, side, cores[dc] * 2 + xs[odd] % 2, send)
                for steps in ALL:
                    if (steps[3], steps[0] % 2) == (dc, odd):
                        send_first(steps)

        side, send, recv = ((0, send_l, recv_l), (1, send_r, recv_r))[u]
        if u == 0:
            loads[3].wait()
            prepare(0, 0)
        for n, group in enumerate(GROUPS):
            for k in range(2):
                project(u, side, xs[group[k]] if u == 0 else cores[1 - n] * 2 + k, send)
            for steps in ALL:
                if group_of(u, steps) == n:
                    send_to(
                        send.at[u, at(channel(u, steps), 16), :], recv.at[u, at(slot, 16), :],
                        send_sem.at[u, 1], second_sem.at[u, n], steps,
                    )

        if u == 0:
            prepare(1, 0)
            prepare(1, 1)
            for n in (4, 5, 6):
                loads[n].wait()
            for v in range(2):
                w_turn[v, 0] = turned(w_gate_ref[v]).astype(BF16)
                w_turn[v, 1] = turned(w_out_ref[v]).astype(BF16)
        gate[...] = jax.nn.sigmoid(jnp.dot(w_turn[u, 0], normed[...], preferred_element_type=F32))

        def arrived(recv, sem, count):
            some = recv.at[u, pl.ds(0, 16 * count), :]
            pltpu.make_async_copy(some, some, sem).wait()

        def side_by_side(recv, first):
            return swap_halves(recv[u, at(first, 16, 8), :], recv[u, at(first + 8, 16, 8), :])

        for d in (1, 3, 2, 0) if u == 0 else (1, 0):
            if u == 0:
                g = xs[-d % 4]
                arrived(recv_r, first_sem.at[u, d], 32)
                low, high = swap_halves(recv_r[u, at(2 * g, 256), :], recv_r[u, at(2 * g + 1, 256), :])
                right_t[at(g, 128), 0:256] = turned(low).astype(BF16)
                right_t[at(g, 128), 256:512] = turned(high).astype(BF16)
            else:
                g = cores[d]
                arrived(recv_l, first_sem.at[u, d], 64)
                for m in range(4):
                    halves = side_by_side(recv_l, 64 * g + 16 * m)
                    for half in range(2):
                        for c in range(8):
                            left_rows[at(4 * c + 2 * g + half, 16), m * 128 : m * 128 + 128] = halves[half][
                                c * 16 : c * 16 + 16
                            ]

        for n, group in enumerate(GROUPS):
            if u == 0:
                sources = [xs[-d % 4] for d in group]
                arrived(recv_l, second_sem.at[u, n], 64)
                pairs = [
                    swap_halves(recv_l[u, at(2 * g, 256), :], recv_l[u, at(2 * g + 1, 256), :]) for g in sources
                ]
                left = jnp.concatenate(
                    [jnp.concatenate([pair[half] for pair in pairs], axis=1) for half in range(2)], axis=0
                )
                edges = jnp.dot(right_t[...], left, preferred_element_type=F32).astype(BF16)
                for c in range(16):
                    for k in range(2):
                        lanes = slice(k * 128, k * 128 + 128)
                        low, high = swap_halves(
                            edges[c * 32 : c * 32 + 16, lanes], edges[c * 32 + 16 : c * 32 + 32, lanes]
                        )
                        to = (n * 64 + k * 32 + c) * 16
                        send_e[u, to : to + 16, :] = low
                        send_e[u, to + 256 : to + 272, :] = high
            else:
                arrived(recv_r, second_sem.at[u, n], 64)
                g = cores[1 - n]
                pairs = [side_by_side(recv_r, 64 * g + 16 * m) for m in range(4)]
                right = jnp.concatenate(
                    [jnp.concatenate([pair[half] for pair in pairs], axis=1) for half in range(2)], axis=0
                )
                edges = lax.dot_general(
                    right, left_rows[...], (((1,), (1,)), ((), ())), preferred_element_type=F32
                ).astype(BF16)
                first, second = edges[:128], edges[128:]
                for k in range(8):
                    for m in range(4):
                        part = (slice(k * 16, k * 16 + 16), slice(m * 128, m * 128 + 128))
                        low, high = swap_halves(first[part], second[part])
                        to = (n * 64 + k * 8 + 2 * m) * 16
                        send_e[u, to : to + 16, :] = low
                        send_e[u, to + 16 : to + 32, :] = high
            for steps in ALL:
                if group_of(u, steps) == n:
                    pr, pc = device(steps)
                    if u == 0:
                        there = (n * 2 + group.index(-steps[0] % 4)) * 32 + pr % 2 * 16 + pc
                    else:
                        there = n * 64 + (pc // 2) * 8 + pr
                    send_to(
                        send_e.at[u, at(there, 16), :], recv_e.at[u, at(channel(u, (0, 0, 0, 0)), 16), :],
                        send_sem.at[u, 2], edge_sem.at[u, n], steps,
                    )

        gain_out = gain_of(ln_out_ref, u)
        gain_next = gain_of(ln_in_ref, 1)
        for n, group in enumerate(GROUPS):
            arrived(recv_e, edge_sem.at[u, n], 64)
            for k in range(2):
                base = xs[group[k]] * 32 if u == 0 else cores[1 - n] * 64 + k * 32
                for h in range(32):
                    spread_buf[at(base * 3 + h * 3, 8, 2), :] = recv_e[u, at(base + h, 16), :].astype(F32)
        for s in range(16):
            lanes = slice(s * 128, s * 128 + 128)
            scaled = norm_rows(spread_buf[pl.ds(s, 128, stride=24), :], gain_out).astype(BF16)
            update = jnp.dot(w_turn[u, 1], scaled, preferred_element_type=F32)
            updated = tile[:, lanes].astype(F32) + gate[:, lanes] * update
            if u == 0:
                rounded = updated.astype(BF16)
                tile[:, lanes] = rounded
                normed[:, lanes] = norm_rows(rounded.astype(F32), gain_next).astype(BF16)
            else:
                block = jnp.transpose(updated)
                flat[pl.ds(s, 64, stride=40), :] = block[:64]
                flat[pl.ds(16 + s, 64, stride=40), :] = block[64:]
    for ii in range(64):
        out_ref[ii] = flat[ii * 40 : ii * 40 + 32, :].astype(BF16)

    for u in range(2):
        for n in range(3):
            sent = send_e.at[u, pl.ds(0, 127 * 16), :]
            pltpu.make_async_copy(sent, sent, send_sem.at[u, n]).wait()


def local(*args):
    tokens = pltpu.VMEM((2, 2048, 128), BF16)
    return pl.pallas_call(
        kernel,
        out_shape=jax.ShapeDtypeStruct((64, 32, 128), BF16),
        in_specs=[pl.BlockSpec(memory_space=pl.ANY)] * 7,
        out_specs=pl.BlockSpec(memory_space=pltpu.VMEM),
        scratch_shapes=[pltpu.VMEM(arg.shape, arg.dtype) for arg in args]
        + [
            pltpu.VMEM((64 * 40, 128), F32),
            pltpu.VMEM((128, 2048), BF16),
            pltpu.VMEM((128, 2048), BF16),
            pltpu.VMEM((128, 2048), F32),
            pltpu.VMEM((128 * 24, 128), F32),
            pltpu.VMEM((2, 2, 4, 64, 128), BF16),
            pltpu.VMEM((2, 2, 128, 128), BF16),
            pltpu.VMEM((512, 512), BF16),
            pltpu.VMEM((512, 512), BF16),
            tokens, tokens, tokens, tokens, tokens, tokens,
            pltpu.SemaphoreType.DMA((7,)),
            pltpu.SemaphoreType.DMA((2, 3)),
            pltpu.SemaphoreType.DMA((2, 4)),
            pltpu.SemaphoreType.DMA((2, 2)),
            pltpu.SemaphoreType.DMA((2, 2)),
        ],
        compiler_params=pltpu.CompilerParams(
            collective_id=0, has_side_effects=True, vmem_limit_bytes=48 << 20
        ),
        name="triangle",
    )(*[pltpu.with_memory_space_constraint(arg, pltpu.HBM) for arg in args])


def solution(mesh):
    return jax.shard_map(
        local,
        mesh=mesh,
        in_specs=(P("row", "col", None), P(), P(), P(), P(), P(), P()),
        out_specs=P("row", "col", None),
        check_vma=False,
    )
```

```python
import itertools

import jax
import jax.numpy as jnp
from jax import lax
from jax.experimental import pallas as pl
from jax.experimental.pallas import tpu as pltpu
from jax.sharding import PartitionSpec as P


MESH = pl.DeviceIdType.MESH
F32, BF16 = jnp.float32, jnp.bfloat16
EPS = 1e-05
GROUPS = ((1, 3), (2, 0))
OTHERS = ((1, 1), (1, 0), (0, 1), (0, 0))


def hops(steps):
    return sum(min(d, 4 - d) for d in steps[:3])


ALL = sorted(itertools.product(range(4), range(4), range(4), range(2)), key=lambda d: (-hops(d), -d[3]))
FAR = [d for d in ALL if hops(d) > 5]
NEAR = [d for d in ALL if hops(d) <= 5]
RELAYS = [(1, 0, 0, 0)]


def norm_rows(values, gain):
    mean = jnp.mean(values, axis=0, keepdims=True)
    centred = values - mean
    spread = jnp.mean(centred * centred, axis=0, keepdims=True)
    return centred * lax.rsqrt(spread + EPS) * gain


def turned(matrix):
    return jnp.transpose(matrix.astype(F32))


def swap_halves(first, second):
    low = jnp.concatenate([first[:, :64], second[:, :64]], axis=1)
    high = jnp.concatenate([first[:, 64:], second[:, 64:]], axis=1)
    return low, high


def at(index, unit, count=1):
    return pl.ds(pl.multiple_of(index * unit, unit), unit * count)


def kernel(
    pair_hbm, ln_in_hbm, w_left_hbm, w_right_hbm, w_gate_hbm, ln_out_hbm, w_out_hbm, out_ref,
    pair_ref, ln_in_ref, w_left_ref, w_right_ref, w_gate_ref, ln_out_ref, w_out_ref,
    flat, tile, normed, gate, spread_buf, w_proj, w_turn, right_t, left_rows,
    send_l, send_r, send_e, recv_l, recv_r, recv_e,
    load_sem, send_sem, first_sem, second_sem, edge_sem, ready,
):
    row, col = lax.axis_index("row"), lax.axis_index("col")
    x, y, z, core = row // 2, ((col // 2) % 2) * 2 + row % 2, col // 4, col % 2
    xs = [(x + d) % 4 for d in range(4)]
    ys = [(y + d) % 4 for d in range(4)]
    zs = [(z + d) % 4 for d in range(4)]
    cores = [core, 1 - core]
    y_low = [v % 2 for v in ys]
    y_high = [(v // 2) * 2 for v in ys]

    def device(steps):
        dx, dy, dz, dc = steps
        return xs[dx] * 2 + y_low[dy], zs[dz] * 4 + y_high[dy] + cores[dc]

    def channel(u, steps):
        dx, dy, dz, dc = steps
        if u == 0:
            return (xs[dx] * 2 + cores[dc]) * 16 + ys[dy] * 4 + zs[dz]
        return (cores[dc] * 2 + xs[dx] % 2) * 32 + (xs[dx] // 2) * 16 + ys[dy] * 4 + zs[dz]

    def group_of(u, steps):
        return 1 - steps[0] % 2 if u == 0 else 1 - steps[3]

    loads = []
    pairs = (
        (pair_hbm, pair_ref), (ln_in_hbm, ln_in_ref), (w_right_hbm, w_right_ref), (w_left_hbm, w_left_ref),
        (w_gate_hbm, w_gate_ref), (ln_out_hbm, ln_out_ref), (w_out_hbm, w_out_ref),
    )
    for n, (src, dst) in enumerate(pairs):
        loads.append(pltpu.make_async_copy(src, dst, load_sem.at[n]))
        loads[-1].start()

    barrier = pltpu.get_barrier_semaphore()
    for steps in NEAR:
        if any(steps):
            pl.semaphore_signal(barrier, inc=1, device_id=device(steps), device_id_type=MESH)

    def prepare(u, side):
        both = turned((w_left_ref, w_right_ref)[side][u]).astype(BF16)
        for j in range(4):
            w_proj[u, side, j, 0:32] = both[32 * j : 32 * j + 32]
            w_proj[u, side, j, 32:64] = both[128 + 32 * j : 160 + 32 * j]

    def gain_of(ref, u):
        return jnp.transpose(jnp.broadcast_to(ref[u : u + 1, :], (128, 128)))

    loads[0].wait()
    loads[1].wait()
    for ii in range(64):
        flat[ii * 40 : ii * 40 + 32, :] = pair_ref[ii].astype(F32)
    gain_in = gain_of(ln_in_ref, 0)
    for s in range(16):
        block = jnp.concatenate(
            [flat[pl.ds(s, 64, stride=40), :], flat[pl.ds(16 + s, 64, stride=40), :]], axis=0
        )
        block = jnp.transpose(block)
        tile[:, s * 128 : s * 128 + 128] = block.astype(BF16)
        normed[:, s * 128 : s * 128 + 128] = norm_rows(block, gain_in).astype(BF16)

    def send_to(src, dst, out_sem, in_sem, steps):
        if any(steps):
            pltpu.make_async_remote_copy(
                src_ref=src, dst_ref=dst, send_sem=out_sem, recv_sem=in_sem,
                device_id=device(steps), device_id_type=MESH,
            ).start()
        else:
            pltpu.make_async_copy(src, dst, in_sem).start()

    def project(u, side, chunk, send):
        for part in range(4):
            p = jnp.dot(
                w_proj[u, side, chunk], normed[:, part * 512 : part * 512 + 512], preferred_element_type=F32
            )
            value = jax.nn.sigmoid(p[:32]) * p[32:]
            for s in range(4):
                spread_buf[pl.ds(part * 4 + s, 32, stride=24), :] = value[:, s * 128 : s * 128 + 128]
        for h in range(32):
            send[u, at(chunk * 32 + h, 16), :] = spread_buf[h * 24 : h * 24 + 16, :].astype(BF16)

    loads[2].wait()
    prepare(0, 1)

    def project_all(j, carry):
        project(0, 1, j, send_r)
        return carry

    lax.fori_loop(0, 4, project_all, 0)
    pl.semaphore_wait(barrier, len(NEAR) - 1)
    for steps in RELAYS:
        pl.semaphore_signal(ready, inc=1, device_id=device(steps), device_id_type=MESH)

    for u in range(2):
        slot = (row * 16 + col, core * 64 + row * 8 + col // 2)[u]
        side, send, recv = ((1, send_r, recv_r), (0, send_l, recv_l))[u]

        first, first_recv = send, recv

        def send_first(steps):
            send_to(
                first.at[u, at(channel(u, steps), 16), :], first_recv.at[u, at(slot, 16), :],
                send_sem.at[u, 0], first_sem.at[u, steps[3 * u]], steps,
            )

        if u == 0:
            for steps in NEAR:
                send_first(steps)
        else:
            for dc, odd in OTHERS:
                project(u, side, cores[dc] * 2 + xs[odd] % 2, send)
                for steps in ALL:
                    if (steps[3], steps[0] % 2) == (dc, odd):
                        send_first(steps)

        side, send, recv = ((0, send_l, recv_l), (1, send_r, recv_r))[u]
        def send_second(n, some):
            for steps in some:
                if group_of(u, steps) == n:
                    send_to(
                        send.at[u, at(channel(u, steps), 16), :], recv.at[u, at(slot, 16), :],
                        send_sem.at[u, 1], second_sem.at[u, n], steps,
                    )

        if u == 0:
            loads[3].wait()
            prepare(0, 0)
            for k in range(2):
                project(u, side, xs[GROUPS[0][k]], send)
            pl.semaphore_wait(ready, len(RELAYS))
            for steps in FAR:
                send_first(steps)
            send_second(0, ALL)
            for k in range(2):
                project(u, side, xs[GROUPS[1][k]], send)
            send_second(1, ALL)
        else:
            for n in range(2):
                for k in range(2):
                    project(u, side, cores[1 - n] * 2 + k, send)
                send_second(n, ALL)

        if u == 0:
            prepare(1, 0)
            prepare(1, 1)
            for n in (4, 5, 6):
                loads[n].wait()
            for v in range(2):
                w_turn[v, 0] = turned(w_gate_ref[v]).astype(BF16)
                w_turn[v, 1] = turned(w_out_ref[v]).astype(BF16)
        gate[...] = jax.nn.sigmoid(jnp.dot(w_turn[u, 0], normed[...], preferred_element_type=F32))

        def arrived(recv, sem, count):
            some = recv.at[u, pl.ds(0, 16 * count), :]
            pltpu.make_async_copy(some, some, sem).wait()

        def side_by_side(recv, first):
            return swap_halves(recv[u, at(first, 16, 8), :], recv[u, at(first + 8, 16, 8), :])

        for d in (1, 3, 2, 0) if u == 0 else (1, 0):
            if u == 0:
                g = xs[-d % 4]
                arrived(recv_r, first_sem.at[u, d], 32)
                low, high = swap_halves(recv_r[u, at(2 * g, 256), :], recv_r[u, at(2 * g + 1, 256), :])
                right_t[at(g, 128), 0:256] = turned(low).astype(BF16)
                right_t[at(g, 128), 256:512] = turned(high).astype(BF16)
            else:
                g = cores[d]
                arrived(recv_l, first_sem.at[u, d], 64)
                for m in range(4):
                    halves = side_by_side(recv_l, 64 * g + 16 * m)
                    for half in range(2):
                        for c in range(8):
                            left_rows[at(4 * c + 2 * g + half, 16), m * 128 : m * 128 + 128] = halves[half][
                                c * 16 : c * 16 + 16
                            ]

        for n, group in enumerate(GROUPS):
            if u == 0:
                sources = [xs[-d % 4] for d in group]
                arrived(recv_l, second_sem.at[u, n], 64)
                pairs = [
                    swap_halves(recv_l[u, at(2 * g, 256), :], recv_l[u, at(2 * g + 1, 256), :]) for g in sources
                ]
                left = jnp.concatenate(
                    [jnp.concatenate([pair[half] for pair in pairs], axis=1) for half in range(2)], axis=0
                )
                edges = jnp.dot(right_t[...], left, preferred_element_type=F32).astype(BF16)
                for c in range(16):
                    for k in range(2):
                        lanes = slice(k * 128, k * 128 + 128)
                        low, high = swap_halves(
                            edges[c * 32 : c * 32 + 16, lanes], edges[c * 32 + 16 : c * 32 + 32, lanes]
                        )
                        to = (n * 64 + k * 32 + c) * 16
                        send_e[u, to : to + 16, :] = low
                        send_e[u, to + 256 : to + 272, :] = high
            else:
                arrived(recv_r, second_sem.at[u, n], 64)
                g = cores[1 - n]
                pairs = [side_by_side(recv_r, 64 * g + 16 * m) for m in range(4)]
                right = jnp.concatenate(
                    [jnp.concatenate([pair[half] for pair in pairs], axis=1) for half in range(2)], axis=0
                )
                edges = lax.dot_general(
                    right, left_rows[...], (((1,), (1,)), ((), ())), preferred_element_type=F32
                ).astype(BF16)
                top, bottom = edges[:128], edges[128:]
                for k in range(8):
                    for m in range(4):
                        part = (slice(k * 16, k * 16 + 16), slice(m * 128, m * 128 + 128))
                        low, high = swap_halves(top[part], bottom[part])
                        to = (n * 64 + k * 8 + 2 * m) * 16
                        send_e[u, to : to + 16, :] = low
                        send_e[u, to + 16 : to + 32, :] = high
            for steps in ALL:
                if group_of(u, steps) == n:
                    pr, pc = device(steps)
                    if u == 0:
                        there = (n * 2 + group.index(-steps[0] % 4)) * 32 + pr % 2 * 16 + pc
                    else:
                        there = n * 64 + (pc // 2) * 8 + pr
                    send_to(
                        send_e.at[u, at(there, 16), :], recv_e.at[u, at(channel(u, (0, 0, 0, 0)), 16), :],
                        send_sem.at[u, 2], edge_sem.at[u, n], steps,
                    )

        gain_out = gain_of(ln_out_ref, u)
        gain_next = gain_of(ln_in_ref, 1)
        for n, group in enumerate(GROUPS):
            arrived(recv_e, edge_sem.at[u, n], 64)
            for k in range(2):
                base = xs[group[k]] * 32 if u == 0 else cores[1 - n] * 64 + k * 32
                for h in range(32):
                    spread_buf[at(base * 3 + h * 3, 8, 2), :] = recv_e[u, at(base + h, 16), :].astype(F32)
        for s in range(16):
            lanes = slice(s * 128, s * 128 + 128)
            scaled = norm_rows(spread_buf[pl.ds(s, 128, stride=24), :], gain_out).astype(BF16)
            update = jnp.dot(w_turn[u, 1], scaled, preferred_element_type=F32)
            updated = tile[:, lanes].astype(F32) + gate[:, lanes] * update
            if u == 0:
                rounded = updated.astype(BF16)
                tile[:, lanes] = rounded
                normed[:, lanes] = norm_rows(rounded.astype(F32), gain_next).astype(BF16)
            else:
                block = jnp.transpose(updated)
                flat[pl.ds(s, 64, stride=40), :] = block[:64]
                flat[pl.ds(16 + s, 64, stride=40), :] = block[64:]
    for ii in range(64):
        out_ref[ii] = flat[ii * 40 : ii * 40 + 32, :].astype(BF16)

    for u in range(2):
        for n in range(3):
            sent = send_e.at[u, pl.ds(0, 127 * 16), :]
            pltpu.make_async_copy(sent, sent, send_sem.at[u, n]).wait()


def local(*args):
    tokens = pltpu.VMEM((2, 2048, 128), BF16)
    return pl.pallas_call(
        kernel,
        out_shape=jax.ShapeDtypeStruct((64, 32, 128), BF16),
        in_specs=[pl.BlockSpec(memory_space=pl.ANY)] * 7,
        out_specs=pl.BlockSpec(memory_space=pltpu.VMEM),
        scratch_shapes=[pltpu.VMEM(arg.shape, arg.dtype) for arg in args]
        + [
            pltpu.VMEM((64 * 40, 128), F32),
            pltpu.VMEM((128, 2048), BF16),
            pltpu.VMEM((128, 2048), BF16),
            pltpu.VMEM((128, 2048), F32),
            pltpu.VMEM((128 * 24, 128), F32),
            pltpu.VMEM((2, 2, 4, 64, 128), BF16),
            pltpu.VMEM((2, 2, 128, 128), BF16),
            pltpu.VMEM((512, 512), BF16),
            pltpu.VMEM((512, 512), BF16),
            tokens, tokens, tokens, tokens, tokens, tokens,
            pltpu.SemaphoreType.DMA((7,)),
            pltpu.SemaphoreType.DMA((2, 3)),
            pltpu.SemaphoreType.DMA((2, 4)),
            pltpu.SemaphoreType.DMA((2, 2)),
            pltpu.SemaphoreType.DMA((2, 2)),
            pltpu.SemaphoreType.REGULAR,
        ],
        compiler_params=pltpu.CompilerParams(
            collective_id=0, has_side_effects=True, vmem_limit_bytes=48 << 20
        ),
        name="triangle",
    )(*[pltpu.with_memory_space_constraint(arg, pltpu.HBM) for arg in args])


def solution(mesh):
    return jax.shard_map(
        local,
        mesh=mesh,
        in_specs=(P("row", "col", None), P(), P(), P(), P(), P(), P()),
        out_specs=P("row", "col", None),
        check_vma=False,
    )
```

```python
import itertools

import jax
import jax.numpy as jnp
from jax import lax
from jax.experimental import pallas as pl
from jax.experimental.pallas import tpu as pltpu
from jax.sharding import PartitionSpec as P


MESH = pl.DeviceIdType.MESH
F32, BF16 = jnp.float32, jnp.bfloat16
EPS = 1e-05
GROUPS = ((1, 3), (2, 0))
OTHERS = ((1, 1), (1, 0), (0, 1), (0, 0))


def hops(steps):
    return sum(min(d, 4 - d) for d in steps[:3])


ALL = sorted(itertools.product(range(4), range(4), range(4), range(2)), key=lambda d: (-hops(d), -d[3]))
FAR = [d for d in ALL if hops(d) > 5]
NEAR = [d for d in ALL if hops(d) <= 5]
RELAYS = [(1, 0, 0, 0)]


def norm_rows(values, gain):
    mean = jnp.mean(values, axis=0, keepdims=True)
    centred = values - mean
    spread = jnp.mean(centred * centred, axis=0, keepdims=True)
    return centred * lax.rsqrt(spread + EPS) * gain


def turned(matrix):
    return jnp.transpose(matrix.astype(F32))


def swap_halves(first, second):
    low = jnp.concatenate([first[:, :64], second[:, :64]], axis=1)
    high = jnp.concatenate([first[:, 64:], second[:, 64:]], axis=1)
    return low, high


def at(index, unit, count=1):
    return pl.ds(pl.multiple_of(index * unit, unit), unit * count)


def kernel(
    pair_hbm, ln_in_hbm, w_left_hbm, w_right_hbm, w_gate_hbm, ln_out_hbm, w_out_hbm, out_ref,
    pair_ref, ln_in_ref, w_left_ref, w_right_ref, w_gate_ref, ln_out_ref, w_out_ref,
    flat, tile, normed, gate, spread_buf, w_proj, w_turn, right_t, left_rows,
    send_l, send_r, send_e, recv_l, recv_r, recv_e,
    load_sem, send_sem, first_sem, second_sem, edge_sem, ready,
):
    row, col = lax.axis_index("row"), lax.axis_index("col")
    x, y, z, core = row // 2, ((col // 2) % 2) * 2 + row % 2, col // 4, col % 2
    xs = [(x + d) % 4 for d in range(4)]
    ys = [(y + d) % 4 for d in range(4)]
    zs = [(z + d) % 4 for d in range(4)]
    cores = [core, 1 - core]
    y_low = [v % 2 for v in ys]
    y_high = [(v // 2) * 2 for v in ys]

    def device(steps):
        dx, dy, dz, dc = steps
        return xs[dx] * 2 + y_low[dy], zs[dz] * 4 + y_high[dy] + cores[dc]

    def channel(u, steps):
        dx, dy, dz, dc = steps
        if u == 0:
            return (xs[dx] * 2 + cores[dc]) * 16 + ys[dy] * 4 + zs[dz]
        return (cores[dc] * 2 + xs[dx] % 2) * 32 + (xs[dx] // 2) * 16 + ys[dy] * 4 + zs[dz]

    def group_of(u, steps):
        return 1 - steps[0] % 2 if u == 0 else 1 - steps[3]

    loads = []
    pairs = (
        (pair_hbm, pair_ref), (ln_in_hbm, ln_in_ref), (w_right_hbm, w_right_ref), (w_left_hbm, w_left_ref),
        (w_gate_hbm, w_gate_ref), (ln_out_hbm, ln_out_ref), (w_out_hbm, w_out_ref),
    )
    for n, (src, dst) in enumerate(pairs):
        loads.append(pltpu.make_async_copy(src, dst, load_sem.at[n]))
        loads[-1].start()

    barrier = pltpu.get_barrier_semaphore()
    for steps in NEAR:
        if any(steps):
            pl.semaphore_signal(barrier, inc=1, device_id=device(steps), device_id_type=MESH)

    def prepare(u, side):
        both = turned((w_left_ref, w_right_ref)[side][u]).astype(BF16)
        for j in range(4):
            w_proj[u, side, j, 0:32] = both[32 * j : 32 * j + 32]
            w_proj[u, side, j, 32:64] = both[128 + 32 * j : 160 + 32 * j]

    def gain_of(ref, u):
        return jnp.transpose(jnp.broadcast_to(ref[u : u + 1, :], (128, 128)))

    loads[0].wait()
    loads[1].wait()
    for ii in range(64):
        flat[ii * 40 : ii * 40 + 32, :] = pair_ref[ii].astype(F32)
    gain_in = gain_of(ln_in_ref, 0)
    for s in range(16):
        block = jnp.concatenate(
            [flat[pl.ds(s, 64, stride=40), :], flat[pl.ds(16 + s, 64, stride=40), :]], axis=0
        )
        block = jnp.transpose(block)
        tile[:, s * 128 : s * 128 + 128] = block.astype(BF16)
        normed[:, s * 128 : s * 128 + 128] = norm_rows(block, gain_in).astype(BF16)

    def send_to(src, dst, out_sem, in_sem, steps):
        if any(steps):
            pltpu.make_async_remote_copy(
                src_ref=src, dst_ref=dst, send_sem=out_sem, recv_sem=in_sem,
                device_id=device(steps), device_id_type=MESH,
            ).start()
        else:
            pltpu.make_async_copy(src, dst, in_sem).start()

    def project(u, side, chunk, send):
        for part in range(4):
            p = jnp.dot(
                w_proj[u, side, chunk], normed[:, part * 512 : part * 512 + 512], preferred_element_type=F32
            )
            value = jax.nn.sigmoid(p[:32]) * p[32:]
            for s in range(4):
                spread_buf[pl.ds(part * 4 + s, 32, stride=24), :] = value[:, s * 128 : s * 128 + 128]
        for h in range(32):
            send[u, at(chunk * 32 + h, 16), :] = spread_buf[h * 24 : h * 24 + 16, :].astype(BF16)

    loads[2].wait()
    prepare(0, 1)

    def project_all(j, carry):
        project(0, 1, j, send_r)
        return carry

    lax.fori_loop(0, 4, project_all, 0)
    pl.semaphore_wait(barrier, len(NEAR) - 1)
    for steps in RELAYS:
        pl.semaphore_signal(ready, inc=1, device_id=device(steps), device_id_type=MESH)

    for u in range(2):
        slot = (row * 16 + col, core * 64 + row * 8 + col // 2)[u]
        side, send, recv = ((1, send_r, recv_r), (0, send_l, recv_l))[u]

        first, first_recv = send, recv

        def send_first(steps):
            send_to(
                first.at[u, at(channel(u, steps), 16), :], first_recv.at[u, at(slot, 16), :],
                send_sem.at[u, 0], first_sem.at[u, steps[3 * u]], steps,
            )

        if u == 0:
            for steps in NEAR:
                send_first(steps)
        else:
            for dc, odd in OTHERS:
                project(u, side, cores[dc] * 2 + xs[odd] % 2, send)
                for steps in ALL:
                    if (steps[3], steps[0] % 2) == (dc, odd):
                        send_first(steps)

        side, send, recv = ((0, send_l, recv_l), (1, send_r, recv_r))[u]
        def send_second(n, some):
            for steps in some:
                if group_of(u, steps) == n:
                    send_to(
                        send.at[u, at(channel(u, steps), 16), :], recv.at[u, at(slot, 16), :],
                        send_sem.at[u, 1], second_sem.at[u, n], steps,
                    )

        if u == 0:
            loads[3].wait()
            prepare(0, 0)
            for k in range(2):
                project(u, side, xs[GROUPS[0][k]], send)
            pl.semaphore_wait(ready, len(RELAYS))
            for steps in FAR:
                send_first(steps)
            send_second(0, ALL)
            for k in range(2):
                project(u, side, xs[GROUPS[1][k]], send)
            send_second(1, ALL)
        else:
            for n in range(2):
                for k in range(2):
                    project(u, side, cores[1 - n] * 2 + k, send)
                send_second(n, ALL)

        if u == 0:
            prepare(1, 0)
            prepare(1, 1)
            for n in (4, 5, 6):
                loads[n].wait()
            for v in range(2):
                w_turn[v, 0] = turned(w_gate_ref[v]).astype(BF16)
                w_turn[v, 1] = turned(w_out_ref[v]).astype(BF16)
        gate[...] = jax.nn.sigmoid(jnp.dot(w_turn[u, 0], normed[...], preferred_element_type=F32))

        def arrived(recv, sem, count):
            some = recv.at[u, pl.ds(0, 16 * count), :]
            pltpu.make_async_copy(some, some, sem).wait()

        def side_by_side(recv, first):
            return swap_halves(recv[u, at(first, 16, 8), :], recv[u, at(first + 8, 16, 8), :])

        for d in (1, 3, 2, 0) if u == 0 else (1, 0):
            if u == 0:
                g = xs[-d % 4]
                arrived(recv_r, first_sem.at[u, d], 32)
                low, high = swap_halves(recv_r[u, at(2 * g, 256), :], recv_r[u, at(2 * g + 1, 256), :])
                right_t[at(g, 128), 0:256] = turned(low).astype(BF16)
                right_t[at(g, 128), 256:512] = turned(high).astype(BF16)
            else:
                g = cores[d]
                arrived(recv_l, first_sem.at[u, d], 64)
                for m in range(4):
                    halves = side_by_side(recv_l, 64 * g + 16 * m)
                    for half in range(2):
                        for c in range(8):
                            left_rows[at(4 * c + 2 * g + half, 16), m * 128 : m * 128 + 128] = halves[half][
                                c * 16 : c * 16 + 16
                            ]

        def send_edges(n, some, place=0):
            for steps in some:
                if group_of(u, steps) == n:
                    pr, pc = device(steps)
                    if u == 0:
                        there = (n * 2 + GROUPS[n].index(-steps[0] % 4)) * 32 + pr % 2 * 16 + place * 4 + pc % 4
                    else:
                        there = n * 64 + (pc // 2) * 8 + pr
                    send_to(
                        send_e.at[u, at(there, 16), :], recv_e.at[u, at(channel(u, (0, 0, 0, 0)), 16), :],
                        send_sem.at[u, 2], edge_sem.at[u, n], steps,
                    )

        for n, group in enumerate(GROUPS):
            if u == 0:
                sources = [xs[-d % 4] for d in group]
                arrived(recv_l, second_sem.at[u, n], 64)
                pairs = [
                    swap_halves(recv_l[u, at(2 * g, 256), :], recv_l[u, at(2 * g + 1, 256), :]) for g in sources
                ]
                left = jnp.concatenate(
                    [jnp.concatenate([pair[half] for pair in pairs], axis=1) for half in range(2)], axis=0
                )
                for place, dz in enumerate((2, 1, 3, 0)):
                    edges = jnp.dot(
                        right_t[at(zs[dz], 128), :], left, preferred_element_type=F32
                    ).astype(BF16)
                    for c in range(4):
                        for k in range(2):
                            lanes = slice(k * 128, k * 128 + 128)
                            low, high = swap_halves(
                                edges[c * 32 : c * 32 + 16, lanes], edges[c * 32 + 16 : c * 32 + 32, lanes]
                            )
                            to = (n * 64 + k * 32 + place * 4 + c) * 16
                            send_e[u, to : to + 16, :] = low
                            send_e[u, to + 256 : to + 272, :] = high
                    send_edges(n, [steps for steps in ALL if steps[2] == dz], place)
            else:
                arrived(recv_r, second_sem.at[u, n], 64)
                g = cores[1 - n]
                pairs = [side_by_side(recv_r, 64 * g + 16 * m) for m in range(4)]
                right = jnp.concatenate(
                    [jnp.concatenate([pair[half] for pair in pairs], axis=1) for half in range(2)], axis=0
                )
                edges = lax.dot_general(
                    right, left_rows[...], (((1,), (1,)), ((), ())), preferred_element_type=F32
                ).astype(BF16)
                top, bottom = edges[:128], edges[128:]
                for k in range(8):
                    for m in range(4):
                        part = (slice(k * 16, k * 16 + 16), slice(m * 128, m * 128 + 128))
                        low, high = swap_halves(top[part], bottom[part])
                        to = (n * 64 + k * 8 + 2 * m) * 16
                        send_e[u, to : to + 16, :] = low
                        send_e[u, to + 16 : to + 32, :] = high
                send_edges(n, ALL)

        gain_out = gain_of(ln_out_ref, u)
        gain_next = gain_of(ln_in_ref, 1)
        for n, group in enumerate(GROUPS):
            arrived(recv_e, edge_sem.at[u, n], 64)
            for k in range(2):
                base = xs[group[k]] * 32 if u == 0 else cores[1 - n] * 64 + k * 32
                for h in range(32):
                    spread_buf[at(base * 3 + h * 3, 8, 2), :] = recv_e[u, at(base + h, 16), :].astype(F32)
        for s in range(16):
            lanes = slice(s * 128, s * 128 + 128)
            scaled = norm_rows(spread_buf[pl.ds(s, 128, stride=24), :], gain_out).astype(BF16)
            update = jnp.dot(w_turn[u, 1], scaled, preferred_element_type=F32)
            updated = tile[:, lanes].astype(F32) + gate[:, lanes] * update
            if u == 0:
                rounded = updated.astype(BF16)
                tile[:, lanes] = rounded
                normed[:, lanes] = norm_rows(rounded.astype(F32), gain_next).astype(BF16)
            else:
                block = jnp.transpose(updated)
                flat[pl.ds(s, 64, stride=40), :] = block[:64]
                flat[pl.ds(16 + s, 64, stride=40), :] = block[64:]
    for ii in range(64):
        out_ref[ii] = flat[ii * 40 : ii * 40 + 32, :].astype(BF16)

    for u in range(2):
        for n in range(3):
            sent = send_e.at[u, pl.ds(0, 127 * 16), :]
            pltpu.make_async_copy(sent, sent, send_sem.at[u, n]).wait()


def local(*args):
    tokens = pltpu.VMEM((2, 2048, 128), BF16)
    return pl.pallas_call(
        kernel,
        out_shape=jax.ShapeDtypeStruct((64, 32, 128), BF16),
        in_specs=[pl.BlockSpec(memory_space=pl.ANY)] * 7,
        out_specs=pl.BlockSpec(memory_space=pltpu.VMEM),
        scratch_shapes=[pltpu.VMEM(arg.shape, arg.dtype) for arg in args]
        + [
            pltpu.VMEM((64 * 40, 128), F32),
            pltpu.VMEM((128, 2048), BF16),
            pltpu.VMEM((128, 2048), BF16),
            pltpu.VMEM((128, 2048), F32),
            pltpu.VMEM((128 * 24, 128), F32),
            pltpu.VMEM((2, 2, 4, 64, 128), BF16),
            pltpu.VMEM((2, 2, 128, 128), BF16),
            pltpu.VMEM((512, 512), BF16),
            pltpu.VMEM((512, 512), BF16),
            tokens, tokens, tokens, tokens, tokens, tokens,
            pltpu.SemaphoreType.DMA((7,)),
            pltpu.SemaphoreType.DMA((2, 3)),
            pltpu.SemaphoreType.DMA((2, 4)),
            pltpu.SemaphoreType.DMA((2, 2)),
            pltpu.SemaphoreType.DMA((2, 2)),
            pltpu.SemaphoreType.REGULAR,
        ],
        compiler_params=pltpu.CompilerParams(
            collective_id=0, has_side_effects=True, vmem_limit_bytes=48 << 20
        ),
        name="triangle",
    )(*[pltpu.with_memory_space_constraint(arg, pltpu.HBM) for arg in args])


def solution(mesh):
    return jax.shard_map(
        local,
        mesh=mesh,
        in_specs=(P("row", "col", None), P(), P(), P(), P(), P(), P()),
        out_specs=P("row", "col", None),
        check_vma=False,
    )
```
